256 devices in a mesh: seq: 64 (over z, x, core), head: 4 (over y).
Axes of the slice: x: 4, y: 4, z: 8, core: 2. Of those that a mesh axis runs over, the one named last changes fastest.
Arguments:
- queries: bfloat16 [16384, 4096], P('seq', 'head'), may hold values from -6 to 6
- key_vectors: bfloat16 [16384, 2, 4096], P('seq', None, 'head'), may hold values from -6 to 6
- values: bfloat16 [16384, 2, 4096], P('seq', None, 'head'), may hold values from -0.59765625 to 0.59765625
- beta_rates: float32 [16384, 64], P('seq', 'head'), may hold values from 0 to 2, as said below
- log_gate: float32 [16384, 32], P('seq', 'head'), may hold values from -0.7 to 0, as said below
- norm_gain: float32 [128], replicated, may hold values from 0.1 to 1.9
- out_weight: bfloat16 [4096, 4096], P('head'), may hold values from -0.09375 to 0.09375
- decode_owner: int32 [2, 32], P(None, 'head'), may hold values from 0 to 63, as said below
Outputs:
- mixed: bfloat16 [16384, 4096], P(('seq', 'head'))
- decode_states: float32 [64, 32, 128, 128], P('seq', 'head')
The draws below stay inside these ranges and needn't reach their ends.
Inputs may be any that keep to these rules, and one draw needn't show every extreme that they name: `beta_rates`: every rate lies strictly between 0 and 2. `log_gate`: every entry is negative. `decode_owner`: every decode device owns at least one head.
All inputs are finite; a program needn't handle non-finite values.
Results may differ from the reference program's by a relative error of at most 0.0065.
Values sent between devices are 32-bit elements; how exact they have to be, the bound alone decides.
A program may use at most 192 MiB of HBM per device.

```python
import math
import jax
import jax.numpy as jnp
from jax import lax

D = 4096
HEAD_TOTAL = 32
K = 128
PROMPT_TOKENS = 16384
DECODE_DEVS = 64
REPLICAS = 2


def head_classes(key, share):
    return jax.random.uniform(jax.random.fold_in(key, 11), (HEAD_TOTAL,)) < share


def draw_beta_rates(key, part):
    share = 0.5
    keeping = head_classes(key, share)
    key = jax.random.fold_in(key, 1)
    first_key, second_key = jax.random.split(key)
    margin = jnp.exp(jax.random.uniform(first_key, (PROMPT_TOKENS, HEAD_TOTAL, 2), jnp.float32, math.log(1e-05), math.log(0.001)))
    slow_rates = 2.0 - margin
    fast_rates = jax.random.uniform(second_key, (PROMPT_TOKENS, HEAD_TOTAL, 2), jnp.float32, 0.2, 1.8)
    picked = jnp.where(keeping[None, :, None], slow_rates, fast_rates)
    return picked.reshape(PROMPT_TOKENS, 2 * HEAD_TOTAL)


def draw_log_gate(key, part):
    share = 0.5
    keeping = head_classes(key, share)
    key = jax.random.fold_in(key, 2)
    key_sequence = jax.random.split(key, 5)
    slow_rate = jnp.exp(jax.random.uniform(key_sequence[0], (HEAD_TOTAL,), jnp.float32, math.log(0.05), math.log(0.5))) / PROMPT_TOKENS
    fast_rate = jnp.exp(jax.random.uniform(key_sequence[1], (HEAD_TOTAL,), jnp.float32, math.log(1.0 / 50.0), math.log(1.0 / 30.0)))
    head_rate = jnp.where(keeping, slow_rate, fast_rate)
    rough = jnp.exp(jax.random.uniform(key_sequence[2], (PROMPT_TOKENS, HEAD_TOTAL), jnp.float32, math.log(0.5), math.log(2.0)))
    steady_state = -head_rate[None, :] * rough
    token_groups = jax.random.uniform(key_sequence[3], (PROMPT_TOKENS, HEAD_TOTAL)) < 3.0 / PROMPT_TOKENS
    removed_part = jnp.log(jax.random.uniform(key_sequence[4], (PROMPT_TOKENS, HEAD_TOTAL), jnp.float32, 0.5, 0.8))
    return jnp.where(token_groups, removed_part, steady_state)


def draw_decode_owner(key, part):
    key = jax.random.fold_in(key, 3)
    slots = jax.random.permutation(key, REPLICAS * HEAD_TOTAL).astype(jnp.int32)
    return (slots % DECODE_DEVS).reshape(REPLICAS, HEAD_TOTAL).astype(jnp.int32)


def block_levels(stream_key, extent, shards, least, high):
    factor_of, own = 1.0, jax.random.fold_in(stream_key, 6)
    for dim, blocks in shards:
        draws = jnp.exp(jax.random.uniform(jax.random.fold_in(own, dim), (blocks,), jnp.float32, least / len(shards), high / len(shards)))
        factor_of = factor_of * jnp.repeat(draws, extent[dim] // blocks).reshape([-1 if axis == dim else 1 for axis in range(len(extent))])
    return factor_of


def gaussian(rng, shape, width, bound, cuts=(), kind=jnp.bfloat16):
    array = jax.random.normal(rng, shape, jnp.float32) * width
    if len(cuts) > 0:
        array = block_levels(rng, shape, cuts, -0.22, 0.18) * array
    return jnp.clip(array, min=-bound, max=bound).astype(kind)


def setup_inputs(seed: int = 0) -> dict:
    splits = jax.random.split(jax.random.key(seed), 9)
    queries = gaussian(splits[0], (PROMPT_TOKENS, HEAD_TOTAL * K), 1.0, 6.0, ((0, 64), (1, 4)))
    key_vectors = gaussian(splits[1], (PROMPT_TOKENS, 2, HEAD_TOTAL * K), 1.0, 6.0, ((0, 64), (2, 4)))
    values = gaussian(splits[2], (PROMPT_TOKENS, 2, HEAD_TOTAL * K), 0.1, 0.59765625, ((0, 64), (2, 4)))
    beta_rates = draw_beta_rates(jax.random.fold_in(splits[8], 71), 0)
    log_gate = draw_log_gate(jax.random.fold_in(splits[8], 71), 0)
    norm_gain = jnp.clip(1.0 + 0.18 * jax.random.normal(splits[5], (K,), jnp.float32), 0.1, 1.9)
    out_weight = gaussian(splits[6], (HEAD_TOTAL * K, D), (HEAD_TOTAL * K) ** -0.5, 0.09375, ((0, 4),))
    decode_owner = draw_decode_owner(jax.random.fold_in(splits[8], 71), 0)
    return {"queries": queries, "key_vectors": key_vectors, "values": values, "beta_rates": beta_rates, "log_gate": log_gate, "norm_gain": norm_gain, "out_weight": out_weight, "decode_owner": decode_owner}


EXACT_PRECISION = lax.Precision.HIGHEST

def reference(queries, key_vectors, values, beta_rates, log_gate, norm_gain, out_weight, decode_owner):
    length = queries.shape[0]
    query_f = queries.astype(jnp.float32).reshape(length, HEAD_TOTAL, K)
    key_f = key_vectors.astype(jnp.float32).reshape(length, 2, HEAD_TOTAL, K)
    key_unit = key_f * lax.rsqrt(lax.optimization_barrier(jnp.sum(key_f * key_f, -1, keepdims=True)) + 1e-06)
    value_f = values.astype(jnp.float32).reshape(length, 2, HEAD_TOTAL, K)
    rate_f = beta_rates.reshape(length, HEAD_TOTAL, 2)
    retain = jnp.exp(log_gate)

    def advance(current_state, inputs):
        present_query, present_key, value_now, rate_now, retain_now = inputs
        current_state = retain_now[:, None, None] * current_state
        for head_branch in range(2):
            readout_value = jnp.einsum('xm,xmo->xo', present_key[head_branch], current_state, precision=EXACT_PRECISION)
            update = rate_now[:, head_branch][:, None] * (value_now[head_branch] - readout_value)
            current_state = current_state + present_key[head_branch][:, :, None] * update[:, None, :]
        result_output = jnp.einsum('xm,xmo->xo', present_query, current_state, precision=EXACT_PRECISION)
        return (current_state, result_output)
    final_state, attended = lax.scan(advance, jnp.zeros((HEAD_TOTAL, K, K), jnp.float32), (query_f, key_unit, value_f, rate_f, retain))
    scaling = lax.rsqrt(lax.optimization_barrier(jnp.mean(attended * attended, -1, keepdims=True)) + 1e-06)
    normed = (attended * scaling * norm_gain).astype(jnp.bfloat16).reshape(length, HEAD_TOTAL * K)
    mixed = jnp.dot(normed, out_weight, preferred_element_type=jnp.float32).astype(jnp.bfloat16)
    owners = jnp.arange(DECODE_DEVS, dtype=jnp.int32)
    picked = jnp.any(decode_owner[None, :, :] == owners[:, None, None], axis=1)
    decode_states = jnp.where(picked[:, :, None, None], final_state[None], 0.0)
    return (mixed, decode_states)
```

```python
import functools
import jax
import jax.numpy as jnp
from jax import lax
from jax.experimental import pallas as pl
from jax.experimental.pallas import tpu as pltpu
from jax.sharding import PartitionSpec as P

K = 128
TB = 64
ROWS = 2 * TB
SUB = 8
F32 = jnp.float32
BF16 = jnp.bfloat16


def split(x):
    hi = x.astype(BF16)
    return hi, (x - hi.astype(F32)).astype(BF16)


def bdot(a, b):
    if a.ndim == 2:
        return lax.dot_general(a, b, (((1,), (0,)), ((), ())), preferred_element_type=F32)
    return lax.dot_general(a, b, (((2,), (1,)), ((0,), (0,))), preferred_element_type=F32)


def mm3(a, b):
    ah, al = a if isinstance(a, tuple) else split(a)
    bh, bl = b if isinstance(b, tuple) else split(b)
    wide = jnp.concatenate([ah, al], axis=-1)
    tall = jnp.concatenate([bh, bh], axis=-2)
    return bdot(wide, tall) + bdot(ah, bl)


def iota(shape, dim):
    return lax.broadcasted_iota(jnp.int32, shape, dim)


def transition_kernel(nb, q_ref, k_ref, v_ref, beta_ref, gate_ref, sp_ref, r_ref, o_ref, run_scr, row_scr):
    h = pl.program_id(0)
    tokens = nb * TB

    @pl.when(h == 0)
    def _():
        gate = gate_ref[...]
        t_i, s_i = iota((tokens, tokens), 0), iota((tokens, tokens), 1)
        same = (t_i // TB) == (s_i // TB)
        upto = jnp.where(same & (s_i <= t_i), 1.0, 0.0).astype(F32)
        run_scr[...] = lax.dot_general(
            upto, gate, (((1,), (0,)), ((), ())), precision=lax.Precision.HIGHEST, preferred_element_type=F32
        )
        t_j, l_j = iota((tokens, nb * ROWS), 0), iota((tokens, nb * ROWS), 1)
        spread = jnp.where(
            ((t_j // TB) == (l_j // ROWS)) & ((t_j % TB) <= (l_j % TB)), 1.0, 0.0
        ).astype(F32)
        row_scr[...] = lax.dot_general(
            gate, spread, (((0,), (0,)), ((), ())), precision=lax.Precision.HIGHEST, preferred_element_type=F32
        )

    heads = gate_ref.shape[1]
    lane_h = iota((tokens, heads), 1)
    run = jnp.sum(jnp.where(lane_h == h, run_scr[...], 0.0), axis=1, keepdims=True).reshape(nb, TB, 1)
    lane_b = iota((tokens, 2 * heads), 1)
    beta = beta_ref[...]
    beta0 = jnp.sum(jnp.where(lane_b == 2 * h, beta, 0.0), axis=1, keepdims=True).reshape(nb, TB, 1)
    beta1 = jnp.sum(jnp.where(lane_b == 2 * h + 1, beta, 0.0), axis=1, keepdims=True).reshape(nb, TB, 1)
    rates = jnp.concatenate([beta0, beta1], axis=1)
    run_rows = jnp.concatenate([run, run], axis=1)
    lane_run = jnp.sum(
        jnp.where(iota((heads, nb * ROWS), 0) == h, row_scr[...], 0.0), axis=0, keepdims=True
    )
    run_lane = jnp.stack([lane_run[:, b * ROWS:(b + 1) * ROWS] for b in range(nb)], axis=0)
    closing = run_lane[:, :, ROWS - 1:ROWS]

    def unit(x):
        x = x.astype(F32)
        return x * lax.rsqrt(jnp.sum(x * x, axis=-1, keepdims=True) + 1e-6)

    k0 = unit(k_ref[0]).reshape(nb, TB, K)
    k1 = unit(k_ref[1]).reshape(nb, TB, K)
    key = jnp.concatenate([k0, k1], axis=1)
    val = jnp.concatenate(
        [v_ref[0].astype(F32).reshape(nb, TB, K), v_ref[1].astype(F32).reshape(nb, TB, K)], axis=1
    )
    query = q_ref[...].astype(F32).reshape(nb, TB, K)
    key_t = jnp.stack([key[b].T for b in range(nb)], axis=0)
    kth, ktl = split(key_t)
    gram = mm3(jnp.concatenate([key, query], axis=1), (kth, ktl))

    row_t, lane_t = iota((TB, ROWS), 0), iota((TB, ROWS), 1) % TB
    seen = lane_t <= row_t
    decay = jnp.where(seen, jnp.exp(jnp.where(seen, run - run_lane, 0.0)), 0.0)
    scores = gram[:, ROWS:] * decay
    r_i, s_i = iota((ROWS, ROWS), 0), iota((ROWS, ROWS), 1)
    r_t, s_t = r_i % TB, s_i % TB
    below = (r_t > s_t) | ((r_t == s_t) & (r_i > s_i))
    system = jnp.where(below, rates * jnp.concatenate([decay, decay], axis=1) * gram[:, :ROWS], 0.0)

    near = (r_t // SUB) == (s_t // SUB)
    folded = jnp.sum(
        jnp.where(near, system, 0.0).reshape(nb, 2, TB // SUB, SUB, ROWS), axis=2
    ).reshape(nb * 2 * SUB, ROWS)
    e_i, e_l = iota((2 * SUB, ROWS), 0), iota((2 * SUB, ROWS), 1)
    eye = jnp.where(((e_i // SUB) == (e_l // TB)) & ((e_i % SUB) == (e_l % SUB)), 1.0, 0.0).astype(F32)
    inv = jnp.broadcast_to(eye, (nb, 2 * SUB, ROWS))
    base = (iota((nb * 2 * SUB, ROWS), 1) % TB) // SUB * SUB
    for i in range(SUB):
        for j in range(2):
            if i == SUB - 1 and j == 1:
                continue
            factor = jnp.take_along_axis(folded, base + (j * TB + i), axis=1, mode="promise_in_bounds")
            factor = factor.reshape(nb, 2 * SUB, ROWS)
            at = j * SUB + i
            inv = inv - factor * inv[:, at:at + 1, :]
    solve = jnp.broadcast_to(
        inv.reshape(nb, 2, 1, SUB, ROWS), (nb, 2, TB // SUB, SUB, ROWS)
    ).reshape(nb, ROWS, ROWS)
    solve = jnp.where(near, solve, 0.0)
    size = SUB
    while size < TB:
        pair = ((r_t // (2 * size)) == (s_t // (2 * size))) & ((r_t // size) > (s_t // size))
        parts = split(solve)
        solve = solve - mm3(parts, mm3(jnp.where(pair, system, 0.0), parts))
        size *= 2

    grown = jnp.exp(run_rows)
    right = jnp.concatenate([rates * val, (rates * grown) * key], axis=2)
    rows = split(mm3(solve, right))
    key_decayed = key_t * jnp.exp(closing - run_lane)
    z = mm3(jnp.concatenate([key_decayed, scores], axis=1), rows)
    k_i, k_j = iota((K, K), 0), iota((K, K), 1)
    ident = jnp.where(k_i == k_j, 1.0, 0.0).astype(F32)
    step = jnp.exp(closing) * ident - z[:, :K, K:]
    reach = jnp.exp(run) * query - z[:, K:, K:]
    carried = jnp.concatenate([z[0, :K, :K], step[0]], axis=1)
    r_ref[0:TB, :] = reach[0]
    o_ref[0:TB, :] = z[0, K:, :K]
    for b in range(1, nb):
        both = mm3(jnp.concatenate([step[b], reach[b]], axis=0), carried)
        o_ref[b * TB:(b + 1) * TB, :] = both[K:, :K] + z[b, K:, :K]
        r_ref[b * TB:(b + 1) * TB, :] = both[K:, K:]
        carried = both[:K] + jnp.concatenate([z[b, :K, :K], jnp.zeros((K, K), F32)], axis=1)
    sp_ref[0] = carried


def transitions(queries, keys, vals, beta_rates, log_gate):
    tokens, width = queries.shape
    heads = log_gate.shape[1]
    nb = tokens // TB
    whole = pl.BlockSpec(memory_space=pltpu.VMEM)
    head_rows = pl.BlockSpec((tokens, K), lambda h: (0, h))
    head_pair = pl.BlockSpec((2, tokens, K), lambda h: (0, 0, h))
    return pl.pallas_call(
        functools.partial(transition_kernel, nb),
        grid=(heads,),
        in_specs=[head_rows, head_pair, head_pair, whole, whole],
        out_specs=[pl.BlockSpec((1, K, 2 * K), lambda h: (h, 0, 0)), head_rows, head_rows],
        out_shape=[
            jax.ShapeDtypeStruct((heads, K, 2 * K), F32),
            jax.ShapeDtypeStruct((tokens, width), F32),
            jax.ShapeDtypeStruct((tokens, width), F32),
        ],
        scratch_shapes=[pltpu.VMEM((tokens, heads), F32), pltpu.VMEM((heads, nb * ROWS), F32)],
        compiler_params=pltpu.CompilerParams(vmem_limit_bytes=48 * 1024 * 1024),
        name="transitions",
    )(queries, keys, vals, beta_rates, log_gate)
MESH = pl.DeviceIdType.MESH


def place(wide_c):
    return jnp.concatenate([wide_c, jnp.zeros((K, K), F32)], axis=1)


def handoff_kernel(
    planes, sp_ref, in_ref, end_ref, gath, pre, from_low, from_high, out_buf,
    send_a, recv_a, send_up, recv_up, send_dn, recv_dn, send_c, recv_c,
):
    heads = sp_ref.shape[0]
    seq, me_head = lax.axis_index("seq"), lax.axis_index("head")
    z, i = seq // heads, lax.rem(seq, heads)
    up = (lax.rem(z + 1, planes) * heads + i, me_head)
    down = (lax.rem(z + planes - 1, planes) * heads + i, me_head)
    n_up, n_dn = from_low.shape[0], from_high.shape[0]

    def peer(offset):
        return lax.rem(i + offset, heads)

    barrier = pltpu.get_barrier_semaphore()
    for offset in range(1, heads):
        pl.semaphore_signal(barrier, inc=1, device_id=(z * heads + peer(offset), me_head), device_id_type=MESH)
    for where in (up, down):
        pl.semaphore_signal(barrier, inc=1, device_id=where, device_id_type=MESH)
    pl.semaphore_wait(barrier, heads + 1)

    own = pltpu.make_async_copy(sp_ref.at[i], gath.at[i], recv_a.at[i])
    own.start()
    first = []
    for offset in range(1, heads):
        other = peer(offset)
        copy = pltpu.make_async_remote_copy(
            src_ref=sp_ref.at[other], dst_ref=gath.at[i], send_sem=send_a.at[offset - 1],
            recv_sem=recv_a.at[i], device_id=(z * heads + other, me_head), device_id_type=MESH,
        )
        copy.start()
        first.append(copy)

    def arrived(src):
        pltpu.make_async_copy(gath.at[src], gath.at[src], recv_a.at[src]).wait()

    arrived(0)
    pre[1] = gath[0]

    def chain(src, _):
        arrived(src)
        later = gath[src]
        pre[src + 1] = mm3(later[:, K:], pre[src]) + place(later[:, :K])
        return 0

    lax.fori_loop(1, heads, chain, 0)

    def hop(src, dst, send, recv, where):
        copy = pltpu.make_async_remote_copy(
            src_ref=src, dst_ref=dst, send_sem=send, recv_sem=recv, device_id=where, device_id_type=MESH
        )
        copy.start()
        return copy

    total = pre.at[heads]
    ups, dns = [], []
    k_i, k_j = iota((K, 2 * K), 0), iota((K, 2 * K), 1)
    acc = jnp.where(k_i + K == k_j, 1.0, 0.0).astype(F32)
    state = jnp.zeros((K, K), F32)
    ups.append(hop(total, from_low.at[0], send_up.at[0], recv_up.at[0], up))
    dns.append(hop(total, from_high.at[0], send_dn.at[0], recv_dn.at[0], down))
    for s in range(1, n_up + 1):
        ups[s - 1].wait_recv()
        if s < n_up:
            ups.append(hop(from_low.at[s - 1], from_low.at[s], send_up.at[s], recv_up.at[s], up))
        if s <= n_dn:
            dns[s - 1].wait_recv()
            if s < n_dn:
                dns.append(hop(from_high.at[s - 1], from_high.at[s], send_dn.at[s], recv_dn.at[s], down))
        earlier = from_low[s - 1]
        if s == 1:
            joined = earlier
        else:
            joined = mm3(acc[:, K:], earlier) + place(acc[:, :K])
        acc = jnp.where(z >= s, joined, acc)
        if s <= n_dn:
            wrapped = from_high[s - 1]
            if s == 1:
                moved = wrapped[:, :K]
            else:
                moved = mm3(wrapped[:, K:], state) + wrapped[:, :K]
            state = jnp.where(z + s >= planes, moved, state)
    start = mm3(acc[:, K:], state) + acc[:, :K]
    start_parts = split(start)

    last = []
    for offset in range(1, heads):
        other = peer(offset)
        part = pre[lax.max(other, 1)]
        moved = mm3(part[:, K:], start_parts) + part[:, :K]
        out_buf[offset - 1] = jnp.where(other == 0, start, moved)
        copy = pltpu.make_async_remote_copy(
            src_ref=out_buf.at[offset - 1], dst_ref=in_ref.at[i], send_sem=send_c.at[offset - 1],
            recv_sem=recv_c.at[i], device_id=(z * heads + other, me_head), device_id_type=MESH,
        )
        copy.start()
        last.append(copy)
    part = pre[lax.max(i, 1)]
    in_ref[i] = jnp.where(i == 0, start, mm3(part[:, K:], start_parts) + part[:, :K])
    part = pre[heads]
    end_ref[...] = mm3(part[:, K:], start_parts) + part[:, :K]
    for offset in range(1, heads):
        other = peer(offset)
        pltpu.make_async_copy(in_ref.at[other], in_ref.at[other], recv_c.at[other]).wait()
    for copy in first + ups + dns + last:
        copy.wait_send()


def handoff(sp, planes):
    heads = sp.shape[0]
    n_up, n_dn = planes // 2, planes - 1 - planes // 2
    dma = pltpu.SemaphoreType.DMA
    whole = pl.BlockSpec(memory_space=pltpu.VMEM)
    return pl.pallas_call(
        functools.partial(handoff_kernel, planes),
        in_specs=[whole],
        out_specs=[whole, whole],
        out_shape=[jax.ShapeDtypeStruct((heads, K, K), F32), jax.ShapeDtypeStruct((K, K), F32)],
        scratch_shapes=[
            pltpu.VMEM((heads, K, 2 * K), F32),
            pltpu.VMEM((heads + 1, K, 2 * K), F32),
            pltpu.VMEM((n_up, K, 2 * K), F32),
            pltpu.VMEM((n_dn, K, 2 * K), F32),
            pltpu.VMEM((heads - 1, K, K), F32),
            dma((heads - 1,)), dma((heads,)), dma((n_up,)), dma((n_up,)), dma((n_dn,)), dma((n_dn,)),
            dma((heads - 1,)), dma((heads,)),
        ],
        compiler_params=pltpu.CompilerParams(
            collective_id=1, has_side_effects=True, vmem_limit_bytes=32 * 1024 * 1024
        ),
        name="handoff",
    )(sp)


def project_kernel(
    planes, r_ref, o_ref, in_ref, gain_ref, w_ref, end_ref, pick_ref, out_ref, states_ref,
    w_buf, normed, part, relay, landed, finals, chosen, taken,
    w_sem, send_sem, relay_sem, land_sem, share_send, share_recv, give_send, give_recv,
):
    chunks, depth, width = w_buf.shape
    half = width // 2
    tokens = r_ref.shape[0]
    ring = part.shape[2]
    rows = tokens // ring
    heads = in_ref.shape[0]
    seq, me = lax.axis_index("seq"), lax.axis_index("head")
    right, left = lax.rem(me + 1, ring), lax.rem(me + ring - 1, ring)
    far = lax.rem(me + 2, ring)
    z, i = seq // heads, lax.rem(seq, heads)
    at_end = z == planes - 1

    def load(c):
        return pltpu.make_async_copy(w_ref.at[:, pl.ds(c * width, width)], w_buf.at[c], w_sem.at[c])

    for c in range(chunks):
        load(c).start()
    barrier = pltpu.get_barrier_semaphore()
    for where in (left, right):
        pl.semaphore_signal(barrier, inc=1, device_id=(seq, where), device_id_type=MESH)

    @pl.when(z != planes - 1)
    def _():
        source = (planes - 1) * heads + i
        pl.semaphore_signal(barrier, inc=1, device_id=(source, me), device_id_type=MESH)

    @pl.when(at_end)
    def _():
        for offset in range(1, heads):
            other = z * heads + lax.rem(i + offset, heads)
            pl.semaphore_signal(barrier, inc=1, device_id=(other, me), device_id_type=MESH)

    def share(offset):
        other = lax.rem(i + offset, heads)
        return pltpu.make_async_remote_copy(
            src_ref=end_ref, dst_ref=finals.at[i], send_sem=share_send.at[offset - 1],
            recv_sem=share_recv.at[i], device_id=(z * heads + other, me), device_id_type=MESH,
        )

    def give(plane):
        return pltpu.make_async_remote_copy(
            src_ref=chosen.at[plane], dst_ref=taken, send_sem=give_send.at[plane],
            recv_sem=give_recv.at[0], device_id=(plane * heads + i, me), device_id_type=MESH,
        )

    gain = gain_ref[...]
    for h in range(heads):
        cols = slice(h * K, (h + 1) * K)
        attended = o_ref[:, cols] + mm3(r_ref[:, cols], in_ref[h])
        scale = lax.rsqrt(jnp.mean(attended * attended, axis=-1, keepdims=True) + 1e-6)
        normed[:, cols] = (attended * scale * gain).astype(BF16)

    @pl.when(at_end)
    def _():
        pl.semaphore_wait(barrier, 2 + heads - 1 + planes - 1)
        finals[i] = end_ref[...]
        for offset in range(1, heads):
            share(offset).start()

    @pl.when(z != planes - 1)
    def _():
        pl.semaphore_wait(barrier, 2)

    def push(src, dst, kind, c, recv, where):
        return pltpu.make_async_remote_copy(
            src_ref=src, dst_ref=dst, send_sem=send_sem.at[c, kind], recv_sem=recv,
            device_id=(seq, where), device_id_type=MESH,
        )

    def far_a(c):
        return push(part.at[c, 0, far], relay.at[c, 0], 0, c, relay_sem.at[c, 0], right)

    def far_b(c):
        return push(part.at[c, 1, far], relay.at[c, 1], 1, c, relay_sem.at[c, 1], left)

    def near_b(c):
        return push(part.at[c, 1, right], landed.at[c, 1], 2, c, land_sem.at[c, 1], right)

    def near_a(c):
        return push(part.at[c, 0, left], landed.at[c, 2], 3, c, land_sem.at[c, 2], left)

    def sum_a(c):
        return push(part.at[c, 0, right], landed.at[c, 0], 4, c, land_sem.at[c, 0], right)

    def sum_b(c):
        return push(part.at[c, 1, left], landed.at[c, 3], 5, c, land_sem.at[c, 3], left)

    def merge(c):
        far_a(c).wait_recv()
        part[c, 0, right] = part[c, 0, right] + relay[c, 0]
        sum_a(c).start()
        far_b(c).wait_recv()
        part[c, 1, left] = part[c, 1, left] + relay[c, 1]
        sum_b(c).start()

    def compute(c):
        load(c).wait()
        got = lax.dot_general(
            normed[...], w_buf[c], (((1,), (0,)), ((), ())), preferred_element_type=F32
        )
        part[c, 0] = got[:, :half].reshape(ring, rows, half)
        part[c, 1] = got[:, half:].reshape(ring, rows, half)
        far_a(c).start()
        far_b(c).start()
        near_b(c).start()
        near_a(c).start()

    compute(0)

    def lap(c, _):
        compute(c)
        merge(c - 1)
        return 0

    lax.fori_loop(1, chunks, lap, 0)
    merge(chunks - 1)

    @pl.when(at_end)
    def _():
        for offset in range(1, heads):
            other = lax.rem(i + offset, heads)
            pltpu.make_async_copy(finals.at[other], finals.at[other], share_recv.at[other]).wait()
        for plane in range(planes):
            total = finals[0] * pick_ref[plane, 0]
            for h in range(1, heads):
                total = total + finals[h] * pick_ref[plane, h]
            if plane < planes - 1:
                chosen[plane] = total
                give(plane).start()
            else:
                taken[...] = total

    def finish(c, _):
        for copy in (sum_a(c), near_b(c), near_a(c), sum_b(c)):
            copy.wait_recv()
        one = part[c, 0, me] + landed[c, 0] + landed[c, 2]
        two = part[c, 1, me] + landed[c, 1] + landed[c, 3]
        out_ref[:, pl.ds(pl.multiple_of(c * width, width), width)] = jnp.concatenate(
            [one, two], axis=1
        ).astype(out_ref.dtype)
        for copy in (far_a(c), far_b(c), near_b(c), near_a(c), sum_a(c), sum_b(c)):
            copy.wait_send()
        return 0

    lax.fori_loop(0, chunks, finish, 0)

    @pl.when(at_end)
    def _():
        for offset in range(1, heads):
            share(offset).wait_send()
        for plane in range(planes - 1):
            give(plane).wait_send()

    @pl.when(z != planes - 1)
    def _():
        give(0).wait_recv()

    for h in range(heads):
        states_ref[0, h] = taken[...] * pick_ref[planes, h]


def project(reach, base, incoming, gain, out_weight, closing, pick, ring, chunks=8):
    tokens = reach.shape[0]
    depth, columns = out_weight.shape
    width = columns // chunks
    rows, half = tokens // ring, width // 2
    planes, heads = pick.shape[0] - 1, pick.shape[1]
    dma = pltpu.SemaphoreType.DMA
    whole = pl.BlockSpec(memory_space=pltpu.VMEM)
    return pl.pallas_call(
        functools.partial(project_kernel, planes),
        in_specs=[
            whole, whole, whole, whole, pl.BlockSpec(memory_space=pl.ANY), whole,
            pl.BlockSpec(memory_space=pltpu.SMEM),
        ],
        out_specs=[whole, whole],
        out_shape=[
            jax.ShapeDtypeStruct((rows, columns), BF16),
            jax.ShapeDtypeStruct((1, heads, K, K), F32),
        ],
        scratch_shapes=[
            pltpu.VMEM((chunks, depth, width), BF16),
            pltpu.VMEM((tokens, depth), BF16),
            pltpu.VMEM((chunks, 2, ring, rows, half), F32),
            pltpu.VMEM((chunks, 2, rows, half), F32),
            pltpu.VMEM((chunks, 4, rows, half), F32),
            pltpu.VMEM((heads, K, K), F32),
            pltpu.VMEM((planes - 1, K, K), F32),
            pltpu.VMEM((K, K), F32),
            dma((chunks,)), dma((chunks, 6)), dma((chunks, 2)), dma((chunks, 4)),
            dma((heads - 1,)), dma((heads,)), dma((planes - 1,)), dma((1,)),
        ],
        compiler_params=pltpu.CompilerParams(
            collective_id=2, has_side_effects=True, vmem_limit_bytes=48 * 1024 * 1024
        ),
        name="project",
    )(reach, base, incoming, gain, out_weight, closing, pick)


def per_device(
    queries, key_vectors, values, beta_rates, log_gate, norm_gain, out_weight, decode_owner
):
    heads = log_gate.shape[1]
    planes = lax.axis_size("seq") // heads
    sp, reach, base = transitions(
        queries, key_vectors.transpose(1, 0, 2), values.transpose(1, 0, 2), beta_rates, log_gate
    )
    incoming, closing = handoff(sp, planes)
    position = lax.axis_index("seq")
    column = jnp.arange(planes) * heads + lax.rem(position, heads)
    targets = jnp.concatenate([column, position[None]])
    pick = jnp.any(decode_owner[None] == targets[:, None, None], axis=1).astype(F32)
    mixed, decode_states = project(
        reach, base, incoming, norm_gain.reshape(1, K), out_weight, closing, pick,
        lax.axis_size("head"),
    )
    return mixed, decode_states


def solution(mesh):
    in_specs = (
        P("seq", "head"), P("seq", None, "head"), P("seq", None, "head"), P("seq", "head"),
        P("seq", "head"), P(), P("head", None), P(None, "head"),
    )
    out_specs = (P(("seq", "head"), None), P("seq", "head", None, None))
    return jax.shard_map(
        per_device, mesh=mesh, in_specs=in_specs, out_specs=out_specs, check_vma=False
    )
```

```python
import functools
import jax
import jax.numpy as jnp
from jax import lax
from jax.experimental import pallas as pl
from jax.experimental.pallas import tpu as pltpu
from jax.sharding import PartitionSpec as P

K = 128
TB = 64
ROWS = 2 * TB
SUB = 8
F32 = jnp.float32
BF16 = jnp.bfloat16


def split(x):
    hi = x.astype(BF16)
    return hi, (x - hi.astype(F32)).astype(BF16)


def bdot(a, b):
    if a.ndim == 2:
        return lax.dot_general(a, b, (((1,), (0,)), ((), ())), preferred_element_type=F32)
    return lax.dot_general(a, b, (((2,), (1,)), ((0,), (0,))), preferred_element_type=F32)


def mm3(a, b):
    ah, al = a if isinstance(a, tuple) else split(a)
    bh, bl = b if isinstance(b, tuple) else split(b)
    wide = jnp.concatenate([ah, al], axis=-1)
    tall = jnp.concatenate([bh, bh], axis=-2)
    return bdot(wide, tall) + bdot(ah, bl)


def iota(shape, dim):
    return lax.broadcasted_iota(jnp.int32, shape, dim)


MESH = pl.DeviceIdType.MESH
PIECES = 2


def place(wide_c):
    return jnp.concatenate([wide_c, jnp.zeros(wide_c.shape, F32)], axis=-1)


def masks():
    r_i, s_i = iota((ROWS, ROWS), 0), iota((ROWS, ROWS), 1)
    return r_i, s_i, r_i % TB, s_i % TB


def decays(run, run_lane):
    seen = iota((TB, ROWS), 1) % TB <= iota((TB, ROWS), 0)
    return jnp.where(seen, jnp.exp(jnp.where(seen, run - run_lane, 0.0)), 0.0)


def invert(system, nb, r_t, s_t):
    near = (r_t // SUB) == (s_t // SUB)
    folded = jnp.sum(
        jnp.where(near, system, 0.0).reshape(nb, 2, TB // SUB, SUB, ROWS), axis=2
    ).reshape(nb * 2 * SUB, ROWS)
    e_i, e_l = iota((2 * SUB, ROWS), 0), iota((2 * SUB, ROWS), 1)
    eye = jnp.where(((e_i // SUB) == (e_l // TB)) & ((e_i % SUB) == (e_l % SUB)), 1.0, 0.0).astype(F32)
    inv = jnp.broadcast_to(eye, (nb, 2 * SUB, ROWS))
    base = (iota((nb * 2 * SUB, ROWS), 1) % TB) // SUB * SUB
    for i in range(SUB):
        for j in range(2):
            if i == SUB - 1 and j == 1:
                continue
            factor = jnp.take_along_axis(folded, base + (j * TB + i), axis=1, mode="promise_in_bounds")
            factor = factor.reshape(nb, 2 * SUB, ROWS)
            at = j * SUB + i
            inv = inv - factor * inv[:, at:at + 1, :]
    solve = jnp.broadcast_to(
        inv.reshape(nb, 2, 1, SUB, ROWS), (nb, 2, TB // SUB, SUB, ROWS)
    ).reshape(nb, ROWS, ROWS)
    solve = jnp.where(near, solve, 0.0)
    size = SUB
    while size < TB:
        pair = ((r_t // (2 * size)) == (s_t // (2 * size))) & ((r_t // size) > (s_t // size))
        parts = split(solve)
        solve = solve - mm3(parts, mm3(jnp.where(pair, system, 0.0), parts))
        size *= 2
    return solve


def whole_kernel(
    planes, q_ref, k_ref, v_ref, beta_ref, gate_ref, gain_ref, w_ref, pick_ref,
    out_ref, taken, q_buf, w_buf, run_scr, row_scr, beta_scr, sp, gath, rows_hi, rows_lo,
    kt_hi, kt_lo, carry, reach_scr, base_scr, from_low, from_high, out_buf, in_buf, end_buf,
    normed, part, relay, landed, finals, chosen,
    q_sem, w_sem, send_a, recv_a, send_up, recv_up, send_dn, recv_dn, send_c, recv_c,
    send_sem, relay_sem, land_sem, share_send, share_recv, give_send, give_recv,
):
    heads, tokens = gate_ref.shape
    nb = tokens // TB
    chunks, depth, width = w_buf.shape
    half = width // 2
    ring = part.shape[2]
    rows = tokens // ring
    seq, me = lax.axis_index("seq"), lax.axis_index("head")
    z, i = seq // heads, lax.rem(seq, heads)
    at_end = z == planes - 1
    up = (lax.rem(z + 1, planes) * heads + i, me)
    down = (lax.rem(z + planes - 1, planes) * heads + i, me)
    n_up, n_dn = from_low.shape[0], from_high.shape[0]
    right, left = lax.rem(me + 1, ring), lax.rem(me + ring - 1, ring)
    far = lax.rem(me + 2, ring)

    def peer(offset):
        return lax.rem(i + offset, heads)

    def load(c):
        return pltpu.make_async_copy(w_ref.at[:, pl.ds(c * width, width)], w_buf.at[c], w_sem.at[c])

    q_load = pltpu.make_async_copy(q_ref, q_buf, q_sem.at[0])
    q_load.start()
    for c in range(chunks):
        load(c).start()

    barrier = pltpu.get_barrier_semaphore()
    for offset in range(1, heads):
        pl.semaphore_signal(barrier, inc=1, device_id=(z * heads + peer(offset), me), device_id_type=MESH)
    for where in (up, down, (seq, right), (seq, left)):
        pl.semaphore_signal(barrier, inc=1, device_id=where, device_id_type=MESH)

    @pl.when(z != planes - 1)
    def _():
        source = (planes - 1) * heads + i
        pl.semaphore_signal(barrier, inc=1, device_id=(source, me), device_id_type=MESH)

    gate = gate_ref[...]
    t_i, s_i = iota((tokens, tokens), 0), iota((tokens, tokens), 1)
    upto = jnp.where(((t_i // TB) == (s_i // TB)) & (s_i <= t_i), 1.0, 0.0).astype(F32)
    run_scr[...] = lax.dot_general(
        upto, gate, (((1,), (1,)), ((), ())), precision=lax.Precision.HIGHEST, preferred_element_type=F32
    )
    t_j, l_j = iota((tokens, nb * ROWS), 0), iota((tokens, nb * ROWS), 1)
    spread = jnp.where(((t_j // TB) == (l_j // ROWS)) & ((t_j % TB) <= (l_j % TB)), 1.0, 0.0).astype(F32)
    row_scr[...] = lax.dot_general(
        gate, spread, (((1,), (0,)), ((), ())), precision=lax.Precision.HIGHEST, preferred_element_type=F32
    )
    same = jnp.where(t_i == s_i, 1.0, 0.0).astype(F32)
    beta_scr[...] = lax.dot_general(
        same, beta_ref[...], (((1,), (1,)), ((), ())), precision=lax.Precision.HIGHEST,
        preferred_element_type=F32,
    )

    def column(ref, h):
        lanes = iota(ref.shape, 1)
        return jnp.sum(jnp.where(lanes == h, ref[...], 0.0), axis=1, keepdims=True).reshape(nb, TB, 1)

    def lane_rows(h):
        picked = jnp.sum(
            jnp.where(iota((heads, nb * ROWS), 0) == h, row_scr[...], 0.0), axis=0, keepdims=True
        )
        return jnp.stack([picked[:, b * ROWS:(b + 1) * ROWS] for b in range(nb)], axis=0)

    def cols(h):
        return pl.ds(pl.multiple_of(h * K, K), K)

    def unit(x):
        x = x.astype(F32)
        return x * lax.rsqrt(jnp.sum(x * x, axis=-1, keepdims=True) + 1e-6)

    def give_a(h, step):
        return pltpu.make_async_remote_copy(
            src_ref=sp.at[h], dst_ref=gath.at[i], send_sem=send_a.at[step],
            recv_sem=recv_a.at[i], device_id=(z * heads + h, me), device_id_type=MESH,
        )

    def transition(step, _):
        h = lax.rem(i + 1 + step, heads)
        run = column(run_scr, h)
        run_lane = lane_rows(h)
        closing = run_lane[:, :, ROWS - 1:ROWS]
        rates = jnp.concatenate([column(beta_scr, 2 * h), column(beta_scr, 2 * h + 1)], axis=1)
        key = jnp.concatenate(
            [unit(k_ref[j, :, cols(h)]).reshape(nb, TB, K) for j in range(2)], axis=1
        )
        val = jnp.concatenate(
            [v_ref[j, :, cols(h)].astype(F32).reshape(nb, TB, K) for j in range(2)], axis=1
        )
        key_t = jnp.stack([key[b].T for b in range(nb)], axis=0)
        kth, ktl = split(key_t)
        kt_hi[h], kt_lo[h] = kth, ktl
        decay = decays(run, run_lane)
        r_i, s_i, r_t, s_t = masks()
        below = (r_t > s_t) | ((r_t == s_t) & (r_i > s_i))
        gram = mm3(key, (kth, ktl))
        system = jnp.where(below, rates * jnp.concatenate([decay, decay], axis=1) * gram, 0.0)
        solve = invert(system, nb, r_t, s_t)
        grown = jnp.exp(jnp.concatenate([run, run], axis=1))
        got = split(mm3(solve, jnp.concatenate([rates * val, (rates * grown) * key], axis=2)))
        rows_hi[h], rows_lo[h] = got
        z_rows = mm3(key_t * jnp.exp(closing - run_lane), got)
        k_i, k_j = iota((K, K), 0), iota((K, K), 1)
        ident = jnp.where(k_i == k_j, 1.0, 0.0).astype(F32)
        move = jnp.exp(closing) * ident - z_rows[:, :, K:]
        state = jnp.concatenate([z_rows[0, :, :K], move[0]], axis=1)
        for b in range(1, nb):
            carry[h, b - 1] = state
            state = mm3(move[b], state) + place(z_rows[b, :, :K])
        sp[h] = state

        @pl.when((step == 0) & at_end)
        def _():
            pl.semaphore_wait(barrier, heads + 3 + planes - 1)

        @pl.when((step == 0) & (z != planes - 1))
        def _():
            pl.semaphore_wait(barrier, heads + 3)

        @pl.when(step < heads - 1)
        def _():
            give_a(h, step).start()

        @pl.when(step == heads - 1)
        def _():
            gath[h] = state

        return 0

    lax.fori_loop(0, heads, transition, 0)

    def reaches(h, _):
        run = column(run_scr, h)
        query = q_buf[:, cols(h)].astype(F32).reshape(nb, TB, K)
        scores = mm3(query, (kt_hi[h], kt_lo[h])) * decays(run, lane_rows(h))
        z_out = mm3(scores, (rows_hi[h], rows_lo[h]))
        reach = jnp.exp(run) * query - z_out[:, :, K:]
        base_scr[0:TB, cols(h)] = z_out[0, :, :K]
        reach_scr[0:TB, cols(h)] = reach[0]
        both = mm3(reach[1:], carry[h])
        base_scr[TB:, cols(h)] = (both[:, :, :K] + z_out[1:, :, :K]).reshape(tokens - TB, K)
        reach_scr[TB:, cols(h)] = both[:, :, K:].reshape(tokens - TB, K)
        return 0

    for src in range(heads):
        @pl.when(src != i)
        def _():
            pltpu.make_async_copy(gath.at[src], gath.at[src], recv_a.at[src]).wait()
    size = 1
    while size < heads:
        for begin in range(0, heads, 2 * size):
            lo, hi = begin + size, begin + 2 * size
            later = gath[lo:hi]
            joined = mm3(later[:, :, K:].reshape(size * K, K), gath[lo - 1]).reshape(size, K, 2 * K)
            gath[lo:hi] = joined + place(later[:, :, :K])
        size *= 2

    bit = K // PIECES

    def hop(s, p, upward):
        slots = from_low if upward else from_high
        src = gath.at[heads - 1] if s == 0 else slots.at[s - 1]
        send, recv = (send_up, recv_up) if upward else (send_dn, recv_dn)
        lines = pl.ds(p * bit, bit)
        return pltpu.make_async_remote_copy(
            src_ref=src.at[lines], dst_ref=slots.at[s, lines], send_sem=send.at[s, p],
            recv_sem=recv.at[s, p], device_id=up if upward else down, device_id_type=MESH,
        )

    for p in range(PIECES):
        hop(0, p, True).start()
        hop(0, p, False).start()
    q_load.wait()
    k_i, k_j = iota((K, 2 * K), 0), iota((K, 2 * K), 1)
    acc = jnp.where(k_i + K == k_j, 1.0, 0.0).astype(F32)
    state = jnp.zeros((K, K), F32)
    each = heads // n_up
    for s in range(n_up):
        lax.fori_loop(s * each, (s + 1) * each, reaches, 0)
        for p in range(PIECES):
            hop(s, p, True).wait_recv()
            if s + 1 < n_up:
                hop(s + 1, p, True).start()
            if s < n_dn:
                hop(s, p, False).wait_recv()
                if s + 1 < n_dn:
                    hop(s + 1, p, False).start()
        earlier = from_low[s]
        joined = earlier if s == 0 else mm3(acc[:, K:], earlier) + place(acc[:, :K])
        acc = jnp.where(z >= s + 1, joined, acc)
        if s < n_dn:
            wrapped = from_high[s]
            moved = wrapped[:, :K] if s == 0 else mm3(wrapped[:, K:], state) + wrapped[:, :K]
            state = jnp.where(z + s + 1 >= planes, moved, state)
    start = mm3(acc[:, K:], state) + acc[:, :K]

    prefix = gath[...]
    spread_out = mm3(prefix[:, :, K:].reshape(heads * K, K), start).reshape(heads, K, K) + prefix[:, :, :K]
    out_buf[0] = start
    out_buf[1:] = spread_out[:heads - 1]
    end_buf[...] = spread_out[heads - 1]

    def give_c(offset):
        other = peer(offset)
        return pltpu.make_async_remote_copy(
            src_ref=out_buf.at[other], dst_ref=in_buf.at[i], send_sem=send_c.at[offset - 1],
            recv_sem=recv_c.at[i], device_id=(z * heads + other, me), device_id_type=MESH,
        )

    def share(offset):
        other = peer(offset)
        return pltpu.make_async_remote_copy(
            src_ref=end_buf, dst_ref=finals.at[i], send_sem=share_send.at[offset - 1],
            recv_sem=share_recv.at[i], device_id=(z * heads + other, me), device_id_type=MESH,
        )

    def give(plane):
        return pltpu.make_async_remote_copy(
            src_ref=chosen.at[plane], dst_ref=taken, send_sem=give_send.at[plane],
            recv_sem=give_recv.at[0], device_id=(plane * heads + i, me), device_id_type=MESH,
        )

    for offset in range(1, heads):
        give_c(offset).start()
    in_buf[i] = out_buf[i]

    @pl.when(at_end)
    def _():
        finals[i] = end_buf[...]
        for offset in range(1, heads):
            share(offset).start()

    gain = gain_ref[...]

    def attend(offset, _):
        h = peer(offset)

        @pl.when(offset > 0)
        def _():
            pltpu.make_async_copy(in_buf.at[h], in_buf.at[h], recv_c.at[h]).wait()

        attended = base_scr[:, cols(h)] + mm3(reach_scr[:, cols(h)], in_buf[h])
        scale = lax.rsqrt(jnp.mean(attended * attended, axis=-1, keepdims=True) + 1e-6)
        normed[:, cols(h)] = (attended * scale * gain).astype(BF16)
        return 0

    lax.fori_loop(0, heads, attend, 0)

    def push(src, dst, kind, c, recv, where):
        return pltpu.make_async_remote_copy(
            src_ref=src, dst_ref=dst, send_sem=send_sem.at[c, kind], recv_sem=recv,
            device_id=(seq, where), device_id_type=MESH,
        )

    def far_a(c):
        return push(part.at[c, 0, far], relay.at[c, 0], 0, c, relay_sem.at[c, 0], right)

    def far_b(c):
        return push(part.at[c, 1, far], relay.at[c, 1], 1, c, relay_sem.at[c, 1], left)

    def near_b(c):
        return push(part.at[c, 1, right], landed.at[c, 1], 2, c, land_sem.at[c, 1], right)

    def near_a(c):
        return push(part.at[c, 0, left], landed.at[c, 2], 3, c, land_sem.at[c, 2], left)

    def sum_a(c):
        return push(part.at[c, 0, right], landed.at[c, 0], 4, c, land_sem.at[c, 0], right)

    def sum_b(c):
        return push(part.at[c, 1, left], landed.at[c, 3], 5, c, land_sem.at[c, 3], left)

    def merge(c):
        far_a(c).wait_recv()
        part[c, 0, right] = part[c, 0, right] + relay[c, 0]
        sum_a(c).start()
        far_b(c).wait_recv()
        part[c, 1, left] = part[c, 1, left] + relay[c, 1]
        sum_b(c).start()

    def compute(c):
        load(c).wait()
        got = lax.dot_general(
            normed[...], w_buf[c], (((1,), (0,)), ((), ())), preferred_element_type=F32
        )
        part[c, 0] = got[:, :half].reshape(ring, rows, half)
        part[c, 1] = got[:, half:].reshape(ring, rows, half)
        far_a(c).start()
        far_b(c).start()
        near_b(c).start()
        near_a(c).start()

    compute(0)

    def lap(c, _):
        compute(c)
        merge(c - 1)
        return 0

    lax.fori_loop(1, chunks, lap, 0)
    merge(chunks - 1)

    @pl.when(at_end)
    def _():
        for offset in range(1, heads):
            other = lax.rem(i + offset, heads)
            pltpu.make_async_copy(finals.at[other], finals.at[other], share_recv.at[other]).wait()
        for plane in range(planes):
            total = finals[0] * pick_ref[plane, 0]
            for h in range(1, heads):
                total = total + finals[h] * pick_ref[plane, h]
            if plane < planes - 1:
                chosen[plane] = total
                give(plane).start()
            else:
                taken[...] = total

    def finish(c, _):
        for copy in (sum_a(c), near_b(c), near_a(c), sum_b(c)):
            copy.wait_recv()
        one = part[c, 0, me] + landed[c, 0] + landed[c, 2]
        two = part[c, 1, me] + landed[c, 1] + landed[c, 3]
        out_ref[:, pl.ds(pl.multiple_of(c * width, width), width)] = jnp.concatenate(
            [one, two], axis=1
        ).astype(out_ref.dtype)
        for copy in (far_a(c), far_b(c), near_b(c), near_a(c), sum_a(c), sum_b(c)):
            copy.wait_send()
        return 0

    lax.fori_loop(0, chunks, finish, 0)

    @pl.when(at_end)
    def _():
        for offset in range(1, heads):
            share(offset).wait_send()
        for plane in range(planes - 1):
            give(plane).wait_send()

    @pl.when(z != planes - 1)
    def _():
        give(0).wait_recv()

    for step in range(heads - 1):
        give_a(lax.rem(i + 1 + step, heads), step).wait_send()
        give_c(step + 1).wait_send()
    for p in range(PIECES):
        for s in range(n_up):
            hop(s, p, True).wait_send()
        for s in range(n_dn):
            hop(s, p, False).wait_send()


def whole(queries, keys, vals, beta_rates, log_gate, gain, out_weight, pick, ring, chunks=8):
    tokens, wide = queries.shape
    planes, heads = pick.shape
    nb = tokens // TB
    depth, columns = out_weight.shape
    width = columns // chunks
    rows, half = tokens // ring, width // 2
    n_up, n_dn = planes // 2, planes - 1 - planes // 2
    dma = pltpu.SemaphoreType.DMA
    vmem = pl.BlockSpec(memory_space=pltpu.VMEM)
    outside = pl.BlockSpec(memory_space=pl.ANY)
    pair = (heads, K, 2 * K)
    return pl.pallas_call(
        functools.partial(whole_kernel, planes),
        in_specs=[outside, vmem, vmem, vmem, vmem, vmem, outside, pl.BlockSpec(memory_space=pltpu.SMEM)],
        out_specs=[vmem, vmem],
        out_shape=[jax.ShapeDtypeStruct((rows, columns), BF16), jax.ShapeDtypeStruct((K, K), F32)],
        scratch_shapes=[
            pltpu.VMEM((tokens, wide), BF16),
            pltpu.VMEM((chunks, depth, width), BF16),
            pltpu.VMEM((tokens, heads), F32),
            pltpu.VMEM((heads, nb * ROWS), F32),
            pltpu.VMEM((tokens, 2 * heads), F32),
            pltpu.VMEM(pair, F32),
            pltpu.VMEM(pair, F32),
            pltpu.VMEM((heads, nb, ROWS, 2 * K), BF16),
            pltpu.VMEM((heads, nb, ROWS, 2 * K), BF16),
            pltpu.VMEM((heads, nb, K, ROWS), BF16),
            pltpu.VMEM((heads, nb, K, ROWS), BF16),
            pltpu.VMEM((heads, nb - 1, K, 2 * K), F32),
            pltpu.VMEM((tokens, wide), F32),
            pltpu.VMEM((tokens, wide), F32),
            pltpu.VMEM((n_up, K, 2 * K), F32),
            pltpu.VMEM((n_dn, K, 2 * K), F32),
            pltpu.VMEM((heads, K, K), F32),
            pltpu.VMEM((heads, K, K), F32),
            pltpu.VMEM((K, K), F32),
            pltpu.VMEM((tokens, depth), BF16),
            pltpu.VMEM((chunks, 2, ring, rows, half), F32),
            pltpu.VMEM((chunks, 2, rows, half), F32),
            pltpu.VMEM((chunks, 4, rows, half), F32),
            pltpu.VMEM((heads, K, K), F32),
            pltpu.VMEM((planes - 1, K, K), F32),
            dma((1,)), dma((chunks,)), dma((heads - 1,)), dma((heads,)),
            dma((n_up, PIECES)), dma((n_up, PIECES)), dma((n_dn, PIECES)), dma((n_dn, PIECES)),
            dma((heads - 1,)), dma((heads,)),
            dma((chunks, 6)), dma((chunks, 2)), dma((chunks, 4)),
            dma((heads - 1,)), dma((heads,)), dma((planes - 1,)), dma((1,)),
        ],
        compiler_params=pltpu.CompilerParams(
            collective_id=1, has_side_effects=True, vmem_limit_bytes=50 * 1024 * 1024
        ),
        name="whole",
    )(queries, keys, vals, beta_rates, log_gate, gain, out_weight, pick)


def per_device(
    queries, key_vectors, values, beta_rates, log_gate, norm_gain, out_weight, decode_owner
):
    heads = log_gate.shape[1]
    planes = lax.axis_size("seq") // heads
    position = lax.axis_index("seq")
    column = jnp.arange(planes) * heads + lax.rem(position, heads)
    pick = jnp.any(decode_owner[None] == column[:, None, None], axis=1).astype(F32)
    mixed, taken = whole(
        queries, key_vectors.transpose(1, 0, 2), values.transpose(1, 0, 2), beta_rates.T, log_gate.T,
        norm_gain.reshape(1, K), out_weight, pick, lax.axis_size("head"),
    )
    owned = jnp.any(decode_owner == position, axis=0)
    decode_states = jnp.where(owned[:, None, None], taken[None], 0.0)[None]
    return mixed, decode_states


def solution(mesh):
    in_specs = (
        P("seq", "head"), P("seq", None, "head"), P("seq", None, "head"), P("seq", "head"),
        P("seq", "head"), P(), P("head", None), P(None, "head"),
    )
    out_specs = (P(("seq", "head"), None), P("seq", "head", None, None))
    return jax.shard_map(
        per_device, mesh=mesh, in_specs=in_specs, out_specs=out_specs, check_vma=False
    )
```

```python
import functools
import jax
import jax.numpy as jnp
from jax import lax
from jax.experimental import pallas as pl
from jax.experimental.pallas import tpu as pltpu
from jax.sharding import PartitionSpec as P

K = 128
TB = 64
ROWS = 2 * TB
SUB = 8
F32 = jnp.float32
BF16 = jnp.bfloat16


def split(x):
    hi = x.astype(BF16)
    return hi, (x - hi.astype(F32)).astype(BF16)


def bdot(a, b):
    if a.ndim == 2:
        return lax.dot_general(a, b, (((1,), (0,)), ((), ())), preferred_element_type=F32)
    return lax.dot_general(a, b, (((2,), (1,)), ((0,), (0,))), preferred_element_type=F32)


def mm3(a, b):
    ah, al = a if isinstance(a, tuple) else split(a)
    bh, bl = b if isinstance(b, tuple) else split(b)
    wide = jnp.concatenate([ah, al], axis=-1)
    tall = jnp.concatenate([bh, bh], axis=-2)
    return bdot(wide, tall) + bdot(ah, bl)


def iota(shape, dim):
    return lax.broadcasted_iota(jnp.int32, shape, dim)


MESH = pl.DeviceIdType.MESH
PIECES = 2
GROUP = 2


def place(wide_c):
    return jnp.concatenate([wide_c, jnp.zeros(wide_c.shape, F32)], axis=-1)


def masks():
    r_i, s_i = iota((ROWS, ROWS), 0), iota((ROWS, ROWS), 1)
    return r_i, s_i, r_i % TB, s_i % TB


def decays(run, run_lane):
    seen = iota((TB, ROWS), 1) % TB <= iota((TB, ROWS), 0)
    return jnp.where(seen, jnp.exp(jnp.where(seen, run - run_lane, 0.0)), 0.0)


def invert(system, nb, r_t, s_t):
    near = (r_t // SUB) == (s_t // SUB)
    folded = jnp.sum(
        jnp.where(near, system, 0.0).reshape(nb, 2, TB // SUB, SUB, ROWS), axis=2
    ).reshape(nb * 2 * SUB, ROWS)
    e_i, e_l = iota((2 * SUB, ROWS), 0), iota((2 * SUB, ROWS), 1)
    eye = jnp.where(((e_i // SUB) == (e_l // TB)) & ((e_i % SUB) == (e_l % SUB)), 1.0, 0.0).astype(F32)
    inv = jnp.broadcast_to(eye, (nb, 2 * SUB, ROWS))
    base = (iota((nb * 2 * SUB, ROWS), 1) % TB) // SUB * SUB
    for i in range(SUB):
        for j in range(2):
            if i == SUB - 1 and j == 1:
                continue
            factor = jnp.take_along_axis(folded, base + (j * TB + i), axis=1, mode="promise_in_bounds")
            factor = factor.reshape(nb, 2 * SUB, ROWS)
            at = j * SUB + i
            inv = inv - factor * inv[:, at:at + 1, :]
    solve = jnp.broadcast_to(
        inv.reshape(nb, 2, 1, SUB, ROWS), (nb, 2, TB // SUB, SUB, ROWS)
    ).reshape(nb, ROWS, ROWS)
    solve = jnp.where(near, solve, 0.0)
    size = SUB
    while size < TB:
        pair = ((r_t // (2 * size)) == (s_t // (2 * size))) & ((r_t // size) > (s_t // size))
        parts = split(solve)
        solve = solve - mm3(parts, mm3(jnp.where(pair, system, 0.0), parts))
        size *= 2
    return solve


def whole_kernel(
    planes, q_ref, k_hbm, v_hbm, beta_hbm, gate_hbm, gain_hbm, w_ref, owner_hbm,
    out_ref, states_ref, taken, owner_ref, gain_ref, beta_ref, gate_ref, k_ref, v_ref, q_buf, w_buf, run_scr, row_scr, beta_scr, sp, gath, rows_hi, rows_lo,
    kt_hi, kt_lo, carry, reach_scr, base_scr, from_low, from_high, out_buf, in_buf, end_buf,
    normed, part, relay, landed, finals, chosen,
    q_sem, in_sem, k_sem, w_sem, send_a, recv_a, send_up, recv_up, send_dn, recv_dn, send_c, recv_c,
    send_sem, relay_sem, land_sem, share_send, share_recv, give_send, give_recv,
):
    heads, tokens = gate_ref.shape
    nb = tokens // TB
    chunks, depth, width = w_buf.shape
    half = width // 2
    ring = part.shape[2]
    rows = tokens // ring
    seq, me = lax.axis_index("seq"), lax.axis_index("head")
    z, i = seq // heads, lax.rem(seq, heads)
    at_end = z == planes - 1
    up = (lax.rem(z + 1, planes) * heads + i, me)
    down = (lax.rem(z + planes - 1, planes) * heads + i, me)
    n_up, n_dn = from_low.shape[0], from_high.shape[0]
    right, left = lax.rem(me + 1, ring), lax.rem(me + ring - 1, ring)
    far = lax.rem(me + 2, ring)

    def peer(offset):
        return lax.rem(i + offset, heads)

    def load(c):
        return pltpu.make_async_copy(w_ref.at[:, pl.ds(c * width, width)], w_buf.at[c], w_sem.at[c])

    q_load = pltpu.make_async_copy(q_ref, q_buf, q_sem.at[0])
    small = [
        pltpu.make_async_copy(src, dst, in_sem.at[n])
        for n, (src, dst) in enumerate(
            [(gate_hbm, gate_ref), (beta_hbm, beta_ref), (gain_hbm, gain_ref), (owner_hbm, owner_ref)]
        )
    ]
    pairs = heads // GROUP

    def load_pair(n):
        pair = lax.rem(i // GROUP + 1 + n, pairs)
        lanes = pl.ds(pl.multiple_of(pair * GROUP * K, GROUP * K), GROUP * K)
        return [
            pltpu.make_async_copy(src.at[:, :, lanes], dst.at[pair], k_sem.at[n, j])
            for j, (src, dst) in enumerate([(k_hbm, k_ref), (v_hbm, v_ref)])
        ]

    for copy in small[:2]:
        copy.start()
    for n in range(pairs):
        for copy in load_pair(n):
            copy.start()
    for copy in small[2:]:
        copy.start()
    q_load.start()
    for c in range(chunks):
        load(c).start()

    barrier = pltpu.get_barrier_semaphore()
    for offset in range(1, heads):
        pl.semaphore_signal(barrier, inc=1, device_id=(z * heads + peer(offset), me), device_id_type=MESH)
    for where in (up, down, (seq, right), (seq, left)):
        pl.semaphore_signal(barrier, inc=1, device_id=where, device_id_type=MESH)

    @pl.when(z != planes - 1)
    def _():
        source = (planes - 1) * heads + i
        pl.semaphore_signal(barrier, inc=1, device_id=(source, me), device_id_type=MESH)

    for copy in small:
        copy.wait()
    gate = gate_ref[...]
    t_i, s_i = iota((tokens, tokens), 0), iota((tokens, tokens), 1)
    upto = jnp.where(((t_i // TB) == (s_i // TB)) & (s_i <= t_i), 1.0, 0.0).astype(F32)
    run_scr[...] = lax.dot_general(
        upto, gate, (((1,), (1,)), ((), ())), precision=lax.Precision.HIGHEST, preferred_element_type=F32
    )
    t_j, l_j = iota((tokens, nb * ROWS), 0), iota((tokens, nb * ROWS), 1)
    spread = jnp.where(((t_j // TB) == (l_j // ROWS)) & ((t_j % TB) <= (l_j % TB)), 1.0, 0.0).astype(F32)
    row_scr[...] = lax.dot_general(
        gate, spread, (((1,), (0,)), ((), ())), precision=lax.Precision.HIGHEST, preferred_element_type=F32
    )
    same = jnp.where(t_i == s_i, 1.0, 0.0).astype(F32)
    beta_scr[...] = lax.dot_general(
        same, beta_ref[...], (((1,), (1,)), ((), ())), precision=lax.Precision.HIGHEST,
        preferred_element_type=F32,
    )

    batch = GROUP * nb

    def column(ref, lanes_at):
        lanes = iota(ref.shape, 1)
        got = [
            jnp.sum(jnp.where(lanes == at, ref[...], 0.0), axis=1, keepdims=True).reshape(nb, TB, 1)
            for at in lanes_at
        ]
        return jnp.concatenate(got, axis=0)

    def lane_rows(h0):
        got = []
        for g in range(GROUP):
            picked = jnp.sum(
                jnp.where(iota((heads, nb * ROWS), 0) == h0 + g, row_scr[...], 0.0), axis=0, keepdims=True
            )
            got += [picked[:, b * ROWS:(b + 1) * ROWS] for b in range(nb)]
        return jnp.stack(got, axis=0)

    def group_cols(h0):
        return pl.ds(pl.multiple_of(h0 * K, GROUP * K), GROUP * K)

    def by_head(x):
        return jnp.concatenate([x[:, g * K:(g + 1) * K].reshape(nb, TB, K) for g in range(GROUP)], axis=0)

    def unit(x):
        return x * lax.rsqrt(jnp.sum(x * x, axis=-1, keepdims=True) + 1e-6)

    def give_a(h):
        where = jnp.where(h > i, h - 1, h)
        return pltpu.make_async_remote_copy(
            src_ref=sp.at[h], dst_ref=gath.at[i], send_sem=send_a.at[where],
            recv_sem=recv_a.at[i], device_id=(z * heads + h, me), device_id_type=MESH,
        )

    def transition(step, _):
        pair = lax.rem(i // GROUP + 1 + step, pairs)
        h0 = pair * GROUP
        for src, j in ((k_hbm, 0), (v_hbm, 1)):
            dst = (k_ref, v_ref)[j]
            pltpu.make_async_copy(dst.at[pair], dst.at[pair], k_sem.at[step, j]).wait()
        run = column(run_scr, [h0 + g for g in range(GROUP)])
        run_lane = lane_rows(h0)
        closing = run_lane[:, :, ROWS - 1:ROWS]
        rates = jnp.concatenate(
            [column(beta_scr, [2 * (h0 + g) + j for g in range(GROUP)]) for j in range(2)], axis=1
        )
        key = unit(jnp.concatenate([by_head(k_ref[pair, j].astype(F32)) for j in range(2)], axis=1))
        val = jnp.concatenate([by_head(v_ref[pair, j].astype(F32)) for j in range(2)], axis=1)
        key_t = jnp.stack([key[b].T for b in range(batch)], axis=0)
        kth, ktl = split(key_t)
        kt_hi[pair], kt_lo[pair] = kth, ktl
        decay = decays(run, run_lane)
        r_i, s_i, r_t, s_t = masks()
        below = (r_t > s_t) | ((r_t == s_t) & (r_i > s_i))
        gram = mm3(key, (kth, ktl))
        system = jnp.where(below, rates * jnp.concatenate([decay, decay], axis=1) * gram, 0.0)
        solve = invert(system, batch, r_t, s_t)
        grown = jnp.exp(jnp.concatenate([run, run], axis=1))
        got = split(mm3(solve, jnp.concatenate([rates * val, (rates * grown) * key], axis=2)))
        rows_hi[pair], rows_lo[pair] = got
        z_rows = mm3(key_t * jnp.exp(closing - run_lane), got)
        k_i, k_j = iota((K, K), 0), iota((K, K), 1)
        ident = jnp.where(k_i == k_j, 1.0, 0.0).astype(F32)
        move = (jnp.exp(closing) * ident - z_rows[:, :, K:]).reshape(GROUP, nb, K, K)
        fresh = z_rows[:, :, :K].reshape(GROUP, nb, K, K)
        state = jnp.concatenate([fresh[:, 0], move[:, 0]], axis=2)
        for b in range(1, nb):
            carry[pair, b - 1] = state
            state = mm3(move[:, b], state) + place(fresh[:, b])
        sp[pl.ds(h0, GROUP)] = state

        @pl.when((step == 0) & at_end)
        def _():
            pl.semaphore_wait(barrier, heads + 3 + planes - 1)

        @pl.when((step == 0) & (z != planes - 1))
        def _():
            pl.semaphore_wait(barrier, heads + 3)

        for g in range(GROUP):
            @pl.when(h0 + g != i)
            def _():
                give_a(h0 + g).start()

            @pl.when(h0 + g == i)
            def _():
                gath[i] = state[g]

        return 0

    lax.fori_loop(0, pairs, transition, 0)

    def reaches(pair, _):
        h0 = pair * GROUP
        run = column(run_scr, [h0 + g for g in range(GROUP)])
        query = by_head(q_buf[:, group_cols(h0)].astype(F32))
        scores = mm3(query, (kt_hi[pair], kt_lo[pair])) * decays(run, lane_rows(h0))
        z_out = mm3(scores, (rows_hi[pair], rows_lo[pair])).reshape(GROUP, nb, TB, 2 * K)
        reach = (jnp.exp(run) * query).reshape(GROUP, nb, TB, K) - z_out[..., K:]
        base = [z_out[:, 0, :, :K]]
        whole_reach = [reach[:, 0]]
        for b in range(1, nb):
            both = mm3(reach[:, b], carry[pair, b - 1])
            base.append(both[:, :, :K] + z_out[:, b, :, :K])
            whole_reach.append(both[:, :, K:])
        base_scr[pl.ds(h0, GROUP)] = jnp.concatenate(base, axis=1)
        reach_scr[pl.ds(h0, GROUP)] = jnp.concatenate(whole_reach, axis=1)
        return 0

    for src in range(heads):
        @pl.when(src != i)
        def _():
            pltpu.make_async_copy(gath.at[src], gath.at[src], recv_a.at[src]).wait()
    size = 1
    while size < heads:
        for begin in range(0, heads, 2 * size):
            lo, hi = begin + size, begin + 2 * size
            later = gath[lo:hi]
            joined = mm3(later[:, :, K:].reshape(size * K, K), gath[lo - 1]).reshape(size, K, 2 * K)
            gath[lo:hi] = joined + place(later[:, :, :K])
        size *= 2

    bit = K // PIECES

    def hop(s, p, upward):
        slots = from_low if upward else from_high
        src = gath.at[heads - 1] if s == 0 else slots.at[s - 1]
        send, recv = (send_up, recv_up) if upward else (send_dn, recv_dn)
        lines = pl.ds(p * bit, bit)
        return pltpu.make_async_remote_copy(
            src_ref=src.at[lines], dst_ref=slots.at[s, lines], send_sem=send.at[s, p],
            recv_sem=recv.at[s, p], device_id=up if upward else down, device_id_type=MESH,
        )

    for p in range(PIECES):
        hop(0, p, True).start()
        hop(0, p, False).start()
    q_load.wait()
    k_i, k_j = iota((K, 2 * K), 0), iota((K, 2 * K), 1)
    acc = jnp.where(k_i + K == k_j, 1.0, 0.0).astype(F32)
    state = jnp.zeros((K, K), F32)
    each = pairs // n_up
    for s in range(n_up):
        lax.fori_loop(s * each, (s + 1) * each, reaches, 0)
        for p in range(PIECES):
            hop(s, p, True).wait_recv()
            if s + 1 < n_up:
                hop(s + 1, p, True).start()
            if s < n_dn:
                hop(s, p, False).wait_recv()
                if s + 1 < n_dn:
                    hop(s + 1, p, False).start()
        earlier = from_low[s]
        joined = earlier if s == 0 else mm3(acc[:, K:], earlier) + place(acc[:, :K])
        acc = jnp.where(z >= s + 1, joined, acc)
        if s < n_dn:
            wrapped = from_high[s]
            moved = wrapped[:, :K] if s == 0 else mm3(wrapped[:, K:], state) + wrapped[:, :K]
            state = jnp.where(z + s + 1 >= planes, moved, state)
    start = mm3(acc[:, K:], state) + acc[:, :K]

    prefix = gath[...]
    spread_out = mm3(prefix[:, :, K:].reshape(heads * K, K), start).reshape(heads, K, K) + prefix[:, :, :K]
    out_buf[0] = start
    out_buf[1:] = spread_out[:heads - 1]
    end_buf[...] = spread_out[heads - 1]

    def give_c(offset):
        other = peer(offset)
        return pltpu.make_async_remote_copy(
            src_ref=out_buf.at[other], dst_ref=in_buf.at[i], send_sem=send_c.at[offset - 1],
            recv_sem=recv_c.at[i], device_id=(z * heads + other, me), device_id_type=MESH,
        )

    def share(offset):
        other = peer(offset)
        return pltpu.make_async_remote_copy(
            src_ref=end_buf, dst_ref=finals.at[i], send_sem=share_send.at[offset - 1],
            recv_sem=share_recv.at[i], device_id=(z * heads + other, me), device_id_type=MESH,
        )

    def give(plane):
        return pltpu.make_async_remote_copy(
            src_ref=chosen.at[plane], dst_ref=taken, send_sem=give_send.at[plane],
            recv_sem=give_recv.at[0], device_id=(plane * heads + i, me), device_id_type=MESH,
        )

    for offset in range(1, heads):
        give_c(offset).start()
    in_buf[i] = out_buf[i]

    @pl.when(at_end)
    def _():
        finals[i] = end_buf[...]
        for offset in range(1, heads):
            share(offset).start()

    gain = gain_ref[...]

    def owned(device):
        found = jnp.where(owner_ref[...] == device, 1.0, 0.0).astype(F32)
        return jnp.max(found, axis=0, keepdims=True)


    def attend(step, _):
        pair = lax.rem(i // GROUP + step, pairs)
        h0 = pair * GROUP
        for g in range(GROUP):
            @pl.when(h0 + g != i)
            def _():
                pltpu.make_async_copy(in_buf.at[h0 + g], in_buf.at[h0 + g], recv_c.at[h0 + g]).wait()

        these = pl.ds(h0, GROUP)
        attended = base_scr[these] + mm3(reach_scr[these], in_buf[these])
        scale = lax.rsqrt(jnp.mean(attended * attended, axis=-1, keepdims=True) + 1e-6)
        got = (attended * scale * gain).astype(BF16)
        normed[:, group_cols(h0)] = jnp.concatenate([got[g] for g in range(GROUP)], axis=1)
        return 0

    lax.fori_loop(0, pairs, attend, 0)

    def push(src, dst, kind, c, recv, where):
        return pltpu.make_async_remote_copy(
            src_ref=src, dst_ref=dst, send_sem=send_sem.at[c, kind], recv_sem=recv,
            device_id=(seq, where), device_id_type=MESH,
        )

    def far_a(c):
        return push(part.at[c, 0, far], relay.at[c, 0], 0, c, relay_sem.at[c, 0], right)

    def far_b(c):
        return push(part.at[c, 1, far], relay.at[c, 1], 1, c, relay_sem.at[c, 1], left)

    def near_b(c):
        return push(part.at[c, 1, right], landed.at[c, 1], 2, c, land_sem.at[c, 1], right)

    def near_a(c):
        return push(part.at[c, 0, left], landed.at[c, 2], 3, c, land_sem.at[c, 2], left)

    def sum_a(c):
        return push(part.at[c, 0, right], landed.at[c, 0], 4, c, land_sem.at[c, 0], right)

    def sum_b(c):
        return push(part.at[c, 1, left], landed.at[c, 3], 5, c, land_sem.at[c, 3], left)

    def merge(c):
        far_a(c).wait_recv()
        part[c, 0, right] = part[c, 0, right] + relay[c, 0]
        sum_a(c).start()
        far_b(c).wait_recv()
        part[c, 1, left] = part[c, 1, left] + relay[c, 1]
        sum_b(c).start()
        return 0

    def compute(c):
        load(c).wait()
        got = lax.dot_general(
            normed[...], w_buf[c], (((1,), (0,)), ((), ())), preferred_element_type=F32
        )
        part[c, 0] = got[:, :half].reshape(ring, rows, half)
        part[c, 1] = got[:, half:].reshape(ring, rows, half)
        far_a(c).start()
        far_b(c).start()
        return 0

    lax.fori_loop(0, chunks, lambda c, _: compute(c), 0)

    def near(c, _):
        near_b(c).start()
        near_a(c).start()
        return 0

    lax.fori_loop(0, chunks, near, 0)
    lax.fori_loop(0, chunks, lambda c, _: merge(c), 0)

    @pl.when(at_end)
    def _():
        for offset in range(1, heads):
            other = lax.rem(i + offset, heads)
            pltpu.make_async_copy(finals.at[other], finals.at[other], share_recv.at[other]).wait()
        for plane in range(planes):
            picked = owned(plane * heads + i)
            total = finals[0] * picked[:, 0:1]
            for h in range(1, heads):
                total = total + finals[h] * picked[:, h:h + 1]
            if plane < planes - 1:
                chosen[plane] = total
                give(plane).start()
            else:
                taken[...] = total

    def finish(c, _):
        for copy in (sum_a(c), near_b(c), near_a(c), sum_b(c)):
            copy.wait_recv()
        one = part[c, 0, me] + landed[c, 0] + landed[c, 2]
        two = part[c, 1, me] + landed[c, 1] + landed[c, 3]
        out_ref[:, pl.ds(pl.multiple_of(c * width, width), width)] = jnp.concatenate(
            [one, two], axis=1
        ).astype(out_ref.dtype)
        for copy in (far_a(c), far_b(c), near_b(c), near_a(c), sum_a(c), sum_b(c)):
            copy.wait_send()
        return 0

    lax.fori_loop(0, chunks, finish, 0)

    @pl.when(at_end)
    def _():
        for offset in range(1, heads):
            share(offset).wait_send()
        for plane in range(planes - 1):
            give(plane).wait_send()

    @pl.when(z != planes - 1)
    def _():
        give(0).wait_recv()

    mine = owned(seq)
    for h in range(heads):
        states_ref[0, h] = taken[...] * mine[:, h:h + 1]

    for offset in range(1, heads):
        give_a(peer(offset)).wait_send()
        give_c(offset).wait_send()
    for p in range(PIECES):
        for s in range(n_up):
            hop(s, p, True).wait_send()
        for s in range(n_dn):
            hop(s, p, False).wait_send()


def whole(queries, keys, vals, beta_rates, log_gate, gain, out_weight, owner, planes, ring, chunks=8):
    tokens, wide = queries.shape
    heads = owner.shape[1]
    nb = tokens // TB
    depth, columns = out_weight.shape
    width = columns // chunks
    rows, half = tokens // ring, width // 2
    n_up, n_dn = planes // 2, planes - 1 - planes // 2
    dma = pltpu.SemaphoreType.DMA
    vmem = pl.BlockSpec(memory_space=pltpu.VMEM)
    outside = pl.BlockSpec(memory_space=pl.ANY)
    hbm = pl.BlockSpec(memory_space=pltpu.HBM)
    pair = (heads, K, 2 * K)
    return pl.pallas_call(
        functools.partial(whole_kernel, planes),
        in_specs=[hbm, outside, outside, hbm, hbm, hbm, hbm, hbm],
        out_specs=[vmem, vmem],
        out_shape=[
            jax.ShapeDtypeStruct((rows, columns), BF16),
            jax.ShapeDtypeStruct((1, heads, K, K), F32),
        ],
        scratch_shapes=[
            pltpu.VMEM((K, K), F32),
            pltpu.VMEM(owner.shape, jnp.int32),
            pltpu.VMEM((1, K), F32),
            pltpu.VMEM((2 * heads, tokens), F32),
            pltpu.VMEM((heads, tokens), F32),
            pltpu.VMEM((heads // GROUP, 2, tokens, GROUP * K), BF16),
            pltpu.VMEM((heads // GROUP, 2, tokens, GROUP * K), BF16),
            pltpu.VMEM((tokens, wide), BF16),
            pltpu.VMEM((chunks, depth, width), BF16),
            pltpu.VMEM((tokens, heads), F32),
            pltpu.VMEM((heads, nb * ROWS), F32),
            pltpu.VMEM((tokens, 2 * heads), F32),
            pltpu.VMEM(pair, F32),
            pltpu.VMEM(pair, F32),
            pltpu.VMEM((heads // GROUP, GROUP * nb, ROWS, 2 * K), BF16),
            pltpu.VMEM((heads // GROUP, GROUP * nb, ROWS, 2 * K), BF16),
            pltpu.VMEM((heads // GROUP, GROUP * nb, K, ROWS), BF16),
            pltpu.VMEM((heads // GROUP, GROUP * nb, K, ROWS), BF16),
            pltpu.VMEM((heads // GROUP, nb - 1, GROUP, K, 2 * K), F32),
            pltpu.VMEM((heads, tokens, K), F32),
            pltpu.VMEM((heads, tokens, K), F32),
            pltpu.VMEM((n_up, K, 2 * K), F32),
            pltpu.VMEM((n_dn, K, 2 * K), F32),
            pltpu.VMEM((heads, K, K), F32),
            pltpu.VMEM((heads, K, K), F32),
            pltpu.VMEM((K, K), F32),
            pltpu.VMEM((tokens, depth), BF16),
            pltpu.VMEM((chunks, 2, ring, rows, half), F32),
            pltpu.VMEM((chunks, 2, rows, half), F32),
            pltpu.VMEM((chunks, 4, rows, half), F32),
            pltpu.VMEM((heads, K, K), F32),
            pltpu.VMEM((planes - 1, K, K), F32),
            dma((1,)), dma((4,)), dma((heads // GROUP, 2)), dma((chunks,)), dma((heads - 1,)), dma((heads,)),
            dma((n_up, PIECES)), dma((n_up, PIECES)), dma((n_dn, PIECES)), dma((n_dn, PIECES)),
            dma((heads - 1,)), dma((heads,)),
            dma((chunks, 6)), dma((chunks, 2)), dma((chunks, 4)),
            dma((heads - 1,)), dma((heads,)), dma((planes - 1,)), dma((1,)),
        ],
        compiler_params=pltpu.CompilerParams(
            collective_id=1, has_side_effects=True, vmem_limit_bytes=60 * 1024 * 1024
        ),
        name="whole",
    )(queries, keys, vals, beta_rates, log_gate, gain, out_weight, owner)


def per_device(
    queries, key_vectors, values, beta_rates, log_gate, norm_gain, out_weight, decode_owner
):
    heads = log_gate.shape[1]
    planes = lax.axis_size("seq") // heads
    return whole(
        queries, key_vectors.transpose(1, 0, 2), values.transpose(1, 0, 2), beta_rates.T, log_gate.T,
        norm_gain.reshape(1, K), out_weight, decode_owner, planes, lax.axis_size("head"),
    )


def solution(mesh):
    in_specs = (
        P("seq", "head"), P("seq", None, "head"), P("seq", None, "head"), P("seq", "head"),
        P("seq", "head"), P(), P("head", None), P(None, "head"),
    )
    out_specs = (P(("seq", "head"), None), P("seq", "head", None, None))
    return jax.shard_map(
        per_device, mesh=mesh, in_specs=in_specs, out_specs=out_specs, check_vma=False
    )
```

```python
import functools
import jax
import jax.numpy as jnp
from jax import lax
from jax.experimental import pallas as pl
from jax.experimental.pallas import tpu as pltpu
from jax.sharding import PartitionSpec as P

K = 128
TB = 64
ROWS = 2 * TB
SUB = 8
F32 = jnp.float32
BF16 = jnp.bfloat16


def split(x):
    hi = x.astype(BF16)
    return hi, (x - hi.astype(F32)).astype(BF16)


def bdot(a, b):
    if a.ndim == 2:
        return lax.dot_general(a, b, (((1,), (0,)), ((), ())), preferred_element_type=F32)
    return lax.dot_general(a, b, (((2,), (1,)), ((0,), (0,))), preferred_element_type=F32)


def mm3(a, b):
    ah, al = a if isinstance(a, tuple) else split(a)
    bh, bl = b if isinstance(b, tuple) else split(b)
    wide = jnp.concatenate([ah, al], axis=-1)
    tall = jnp.concatenate([bh, bh], axis=-2)
    return bdot(wide, tall) + bdot(ah, bl)


def iota(shape, dim):
    return lax.broadcasted_iota(jnp.int32, shape, dim)


MESH = pl.DeviceIdType.MESH
PIECES = 2
GROUP = 4


def place(wide_c):
    return jnp.concatenate([wide_c, jnp.zeros(wide_c.shape, F32)], axis=-1)


def masks():
    r_i, s_i = iota((ROWS, ROWS), 0), iota((ROWS, ROWS), 1)
    return r_i, s_i, r_i % TB, s_i % TB


def decays(run, run_lane):
    seen = iota((TB, ROWS), 1) % TB <= iota((TB, ROWS), 0)
    return jnp.where(seen, jnp.exp(jnp.where(seen, run - run_lane, 0.0)), 0.0)


def odd_rows(x, size, which=1):
    groups = x.reshape(x.shape[0], ROWS // (2 * size), 2, size, x.shape[-1])
    return groups[:, :, which].reshape(x.shape[0], ROWS // 2, x.shape[-1])


def among_odd(odd, even, size):
    shape = (odd.shape[0], ROWS // (2 * size), 1, size, odd.shape[-1])
    both = jnp.concatenate([even.reshape(shape), odd.reshape(shape)], axis=2)
    return both.reshape(odd.shape[0], ROWS, odd.shape[-1])


def three(x):
    one = x.astype(BF16).astype(F32)
    two = (x - one).astype(BF16).astype(F32)
    return [one, two, x - one - two]


def invert(system, nb, r_t, s_t):
    near = (r_t // SUB) == (s_t // SUB)
    folded = jnp.sum(
        jnp.where(near, system, 0.0).reshape(nb, 2, TB // SUB, SUB, ROWS), axis=2
    ).reshape(nb * 2 * SUB, ROWS)
    e_i, e_l = iota((2 * SUB, ROWS), 0), iota((2 * SUB, ROWS), 1)
    eye = jnp.where(((e_i // SUB) == (e_l // TB)) & ((e_i % SUB) == (e_l % SUB)), 1.0, 0.0).astype(F32)
    inv = jnp.broadcast_to(eye, (nb, 2 * SUB, ROWS))
    base = (iota((nb * 2 * SUB, ROWS), 1) % TB) // SUB * SUB
    for i in range(SUB):
        for j in range(2):
            if i == SUB - 1 and j == 1:
                continue
            factor = jnp.take_along_axis(folded, base + (j * TB + i), axis=1, mode="promise_in_bounds")
            factor = factor.reshape(nb, 2 * SUB, ROWS)
            at = j * SUB + i
            inv = inv - factor * inv[:, at:at + 1, :]
    solve = jnp.broadcast_to(
        inv.reshape(nb, 2, 1, SUB, ROWS), (nb, 2, TB // SUB, SUB, ROWS)
    ).reshape(nb, ROWS, ROWS)
    solve = jnp.where(near, solve, 0.0)
    size = SUB
    while size < TB:
        pair = ((r_t // (2 * size)) == (s_t // (2 * size))) & ((r_t // size) > (s_t // size))
        later = odd_rows(solve, size)
        crossed = mm3(odd_rows(jnp.where(pair, system, 0.0), size), solve)
        later = later - mm3(later, among_odd(crossed, jnp.zeros_like(crossed), size))
        solve = among_odd(later, odd_rows(solve, size, 0), size)
        size *= 2
    return solve


def whole_kernel(
    planes, q_ref, k_hbm, v_hbm, small_ref, w_ref,
    out_ref, states_ref, taken, k_ref, v_ref, q_buf, w_buf, col_scr, row_scr, sp, gath, rows_hi, rows_lo,
    kt_hi, kt_lo, carry, reach_scr, base_scr, from_low, from_high, out_buf, in_buf, end_buf,
    normed, part, relay, landed, finals, chosen,
    q_sem, k_sem, w_sem, send_a, recv_a, send_up, recv_up, send_dn, recv_dn, send_c, recv_c,
    send_sem, relay_sem, land_sem, share_send, share_recv, give_send, give_recv,
):
    tokens = small_ref.shape[1]
    heads = sp.shape[0]
    nb = tokens // TB
    chunks, depth, width = w_buf.shape
    half = width // 2
    ring = part.shape[2]
    rows = tokens // ring
    seq, me = lax.axis_index("seq"), lax.axis_index("head")
    z, i = seq // heads, lax.rem(seq, heads)
    at_end = z == planes - 1
    up = (lax.rem(z + 1, planes) * heads + i, me)
    down = (lax.rem(z + planes - 1, planes) * heads + i, me)
    n_up, n_dn = from_low.shape[0], from_high.shape[0]
    right, left = lax.rem(me + 1, ring), lax.rem(me + ring - 1, ring)
    far = lax.rem(me + 2, ring)

    def peer(offset):
        return lax.rem(i + offset, heads)

    def load(c):
        return pltpu.make_async_copy(w_ref.at[:, pl.ds(c * width, width)], w_buf.at[c], w_sem.at[c])

    q_load = pltpu.make_async_copy(q_ref, q_buf, q_sem.at[0])
    pairs = heads // GROUP

    def load_head(h):
        dst = pl.ds(h // pairs * K, K)
        return [
            pltpu.make_async_copy(
                src.at[:, :, pl.ds(h * K, K)], buf.at[h % pairs, :, :, dst], k_sem.at[h % pairs, h // pairs, j]
            )
            for j, (src, buf) in enumerate([(k_hbm, k_ref), (v_hbm, v_ref)])
        ]

    for n in range(pairs):
        for g in range(GROUP):
            for copy in load_head(n + pairs * g):
                copy.start()
    q_load.start()
    for c in range(chunks):
        load(c).start()

    barrier = pltpu.get_barrier_semaphore()
    for offset in range(1, heads):
        pl.semaphore_signal(barrier, inc=1, device_id=(z * heads + peer(offset), me), device_id_type=MESH)
    for where in (up, down, (seq, right), (seq, left)):
        pl.semaphore_signal(barrier, inc=1, device_id=where, device_id_type=MESH)

    @pl.when(z != planes - 1)
    def _():
        source = (planes - 1) * heads + i
        pl.semaphore_signal(barrier, inc=1, device_id=(source, me), device_id_type=MESH)

    gate = small_ref[0:heads]
    t_i, s_i = iota((tokens, tokens), 0), iota((tokens, tokens), 1)
    upto = jnp.where(((t_i // TB) == (s_i // TB)) & (s_i <= t_i), 1.0, 0.0).astype(F32)
    run = lax.dot_general(
        gate, upto, (((1,), (1,)), ((), ())), precision=lax.Precision.HIGHEST, preferred_element_type=F32
    )
    terms = jnp.concatenate(three(small_ref[heads:3 * heads]) + three(run), axis=0).astype(BF16)
    same = jnp.where(t_i == s_i, 1.0, 0.0).astype(BF16)
    col_scr[...] = lax.dot_general(
        same, terms, (((1,), (1,)), ((), ())), preferred_element_type=F32
    ).astype(BF16)
    row_scr[...] = jnp.concatenate(
        [run[:, b // 2 * TB:(b // 2 + 1) * TB] for b in range(2 * nb)], axis=1
    )

    batch = GROUP * nb

    def columns(h0, kinds):
        shape = (9 * heads, K)
        at = iota(shape, 0)
        rate_at, run_at = jnp.where(at < 6 * heads, at % (2 * heads), -1), jnp.where(at < 6 * heads, -1, at % heads)
        picks = []
        for kind in kinds:
            for g in range(GROUP):
                hit = (run_at == h0 + pairs * g) if kind == 2 else (rate_at == 2 * (h0 + pairs * g) + kind)
                picks.append(jnp.where(hit, 1.0, 0.0).astype(BF16))
        got = lax.dot_general(
            col_scr[...], jnp.concatenate(picks, axis=1), (((1,), (0,)), ((), ())), preferred_element_type=F32
        )
        tiles = [got[:, n * K:(n + 1) * K].reshape(nb, TB, K) for n in range(len(picks))]
        return [jnp.concatenate(tiles[n:n + GROUP], axis=0) for n in range(0, len(picks), GROUP)]

    def lane_rows(h0):
        got = []
        for g in range(GROUP):
            picked = jnp.sum(
                jnp.where(iota((heads, nb * ROWS), 0) == h0 + pairs * g, row_scr[...], 0.0), axis=0, keepdims=True
            )
            got += [picked[:, b * ROWS:(b + 1) * ROWS] for b in range(nb)]
        return jnp.stack(got, axis=0)

    def head_cols(h):
        return pl.ds(pl.multiple_of(h * K, K), K)

    def by_head(x):
        return jnp.concatenate([x[:, g * K:(g + 1) * K].reshape(nb, TB, K) for g in range(GROUP)], axis=0)

    def unit(x):
        return x * lax.rsqrt(jnp.sum(x * x, axis=-1, keepdims=True) + 1e-6)

    def give_a(h):
        where = jnp.where(h > i, h - 1, h)
        return pltpu.make_async_remote_copy(
            src_ref=sp.at[h], dst_ref=gath.at[i], send_sem=send_a.at[where],
            recv_sem=recv_a.at[i], device_id=(z * heads + h, me), device_id_type=MESH,
        )

    def transition(step, _):
        pair = h0 = step
        for g in range(GROUP):
            for j, buf in enumerate((k_ref, v_ref)):
                here = buf.at[pair, :, :, pl.ds(g * K, K)]
                pltpu.make_async_copy(here, here, k_sem.at[pair, g, j]).wait()
        rate0, rate1, run = columns(h0, (0, 1, 2))
        run_lane = lane_rows(h0)
        closing = run_lane[:, :, ROWS - 1:ROWS]
        rates = jnp.concatenate([rate0, rate1], axis=1)
        key = unit(jnp.concatenate([by_head(k_ref[pair, j].astype(F32)) for j in range(2)], axis=1))
        val = jnp.concatenate([by_head(v_ref[pair, j].astype(F32)) for j in range(2)], axis=1)
        key_t = jnp.stack([key[b].T for b in range(batch)], axis=0)
        kth, ktl = split(key_t)
        kt_hi[pair], kt_lo[pair] = kth, ktl
        decay = decays(run, run_lane)
        r_i, s_i, r_t, s_t = masks()
        below = (r_t > s_t) | ((r_t == s_t) & (r_i > s_i))
        gram = mm3(key, (kth, ktl))
        system = jnp.where(below, rates * jnp.concatenate([decay, decay], axis=1) * gram, 0.0)
        solve = invert(system, batch, r_t, s_t)
        grown = jnp.exp(jnp.concatenate([run, run], axis=1))
        got = split(mm3(solve, jnp.concatenate([rates * val, (rates * grown) * key], axis=2)))
        rows_hi[pair], rows_lo[pair] = got
        z_rows = mm3(key_t * jnp.exp(closing - run_lane), got)
        k_i, k_j = iota((K, K), 0), iota((K, K), 1)
        ident = jnp.where(k_i == k_j, 1.0, 0.0).astype(F32)
        move = (jnp.exp(closing) * ident - z_rows[:, :, K:]).reshape(GROUP, nb, K, K)
        fresh = z_rows[:, :, :K].reshape(GROUP, nb, K, K)
        state = jnp.concatenate([fresh[:, 0], move[:, 0]], axis=2)
        for b in range(1, nb):
            carry[pair, b - 1] = state
            state = mm3(move[:, b], state) + place(fresh[:, b])
        for g in range(GROUP):
            sp[h0 + pairs * g] = state[g]

        @pl.when((step == 0) & at_end)
        def _():
            pl.semaphore_wait(barrier, heads + 3 + planes - 1)

        @pl.when((step == 0) & (z != planes - 1))
        def _():
            pl.semaphore_wait(barrier, heads + 3)

        for g in range(GROUP):
            @pl.when(h0 + pairs * g != i)
            def _():
                give_a(h0 + pairs * g).start()

            @pl.when(h0 + pairs * g == i)
            def _():
                gath[i] = state[g]

        return 0

    lax.fori_loop(0, pairs, transition, 0)

    def reaches(pair, _):
        h0 = pair
        (run,) = columns(h0, (2,))
        query = jnp.concatenate(
            [q_buf[:, head_cols(h0 + pairs * g)].astype(F32).reshape(nb, TB, K) for g in range(GROUP)], axis=0
        )
        scores = mm3(query, (kt_hi[pair], kt_lo[pair])) * decays(run, lane_rows(h0))
        z_out = mm3(scores, (rows_hi[pair], rows_lo[pair])).reshape(GROUP, nb, TB, 2 * K)
        reach = (jnp.exp(run) * query).reshape(GROUP, nb, TB, K) - z_out[..., K:]
        base = [z_out[:, 0, :, :K]]
        whole_reach = [reach[:, 0]]
        for b in range(1, nb):
            both = mm3(reach[:, b], carry[pair, b - 1])
            base.append(both[:, :, :K] + z_out[:, b, :, :K])
            whole_reach.append(both[:, :, K:])
        base_scr[pair] = jnp.concatenate(base, axis=1)
        reach_scr[pair] = jnp.concatenate(whole_reach, axis=1)
        return 0

    early = jnp.where(lax.rem(i, pairs) == 0, 0, pairs)
    q_load.wait()
    lax.fori_loop(0, early, reaches, 0)
    for src in range(heads):
        @pl.when(src != i)
        def _():
            pltpu.make_async_copy(gath.at[src], gath.at[src], recv_a.at[src]).wait()
    size = 1
    while size < heads:
        for begin in range(0, heads, 2 * size):
            lo, hi = begin + size, begin + 2 * size
            later = gath[lo:hi]
            joined = mm3(later[:, :, K:].reshape(size * K, K), gath[lo - 1]).reshape(size, K, 2 * K)
            gath[lo:hi] = joined + place(later[:, :, :K])
        size *= 2

    bit = K // PIECES

    def hop(s, p, upward):
        slots = from_low if upward else from_high
        src = gath.at[heads - 1] if s == 0 else slots.at[s - 1]
        send, recv = (send_up, recv_up) if upward else (send_dn, recv_dn)
        lines = pl.ds(p * bit, bit)
        return pltpu.make_async_remote_copy(
            src_ref=src.at[lines], dst_ref=slots.at[s, lines], send_sem=send.at[s, p],
            recv_sem=recv.at[s, p], device_id=up if upward else down, device_id_type=MESH,
        )

    for p in range(PIECES):
        hop(0, p, True).start()
        hop(0, p, False).start()
    k_i, k_j = iota((K, 2 * K), 0), iota((K, 2 * K), 1)
    acc = jnp.where(k_i + K == k_j, 1.0, 0.0).astype(F32)
    state = jnp.zeros((K, K), F32)
    for s in range(n_up):
        if s == 0:
            lax.fori_loop(early, pairs, reaches, 0)
        for p in range(PIECES):
            hop(s, p, True).wait_recv()
            if s + 1 < n_up:
                hop(s + 1, p, True).start()
            if s < n_dn:
                hop(s, p, False).wait_recv()
                if s + 1 < n_dn:
                    hop(s + 1, p, False).start()
        earlier = from_low[s]
        joined = earlier if s == 0 else mm3(acc[:, K:], earlier) + place(acc[:, :K])
        acc = jnp.where(z >= s + 1, joined, acc)
        if s < n_dn:
            wrapped = from_high[s]
            moved = wrapped[:, :K] if s == 0 else mm3(wrapped[:, K:], state) + wrapped[:, :K]
            state = jnp.where(z + s + 1 >= planes, moved, state)
    start = mm3(acc[:, K:], state) + acc[:, :K]

    prefix = gath[...]
    spread_out = mm3(prefix[:, :, K:].reshape(heads * K, K), start).reshape(heads, K, K) + prefix[:, :, :K]
    out_buf[0] = start
    out_buf[1:] = spread_out[:heads - 1]
    end_buf[...] = spread_out[heads - 1]

    def give_c(offset):
        other = peer(offset)
        return pltpu.make_async_remote_copy(
            src_ref=out_buf.at[other], dst_ref=in_buf.at[lax.rem(i, pairs), i // pairs], send_sem=send_c.at[offset - 1],
            recv_sem=recv_c.at[i], device_id=(z * heads + other, me), device_id_type=MESH,
        )

    def share(offset):
        other = peer(offset)
        return pltpu.make_async_remote_copy(
            src_ref=end_buf, dst_ref=finals.at[i], send_sem=share_send.at[offset - 1],
            recv_sem=share_recv.at[i], device_id=(z * heads + other, me), device_id_type=MESH,
        )

    def give(plane):
        return pltpu.make_async_remote_copy(
            src_ref=chosen.at[plane], dst_ref=taken, send_sem=give_send.at[plane],
            recv_sem=give_recv.at[0], device_id=(plane * heads + i, me), device_id_type=MESH,
        )

    for offset in range(1, heads):
        give_c(offset).start()
    in_buf[lax.rem(i, pairs), i // pairs] = out_buf[i]

    @pl.when(at_end)
    def _():
        finals[i] = end_buf[...]
        for offset in range(1, heads):
            share(offset).start()

    gain = small_ref[3 * heads:3 * heads + 1, 0:K]

    def owned(device):
        owners = small_ref[3 * heads + 1:3 * heads + 3, 0:heads]
        found = jnp.where(owners == lax.convert_element_type(device, F32), 1.0, 0.0).astype(F32)
        return jnp.max(found, axis=0, keepdims=True)


    def attend(step, _):
        for g in range(GROUP):
            h = step + pairs * g

            @pl.when(h != i)
            def _():
                here = in_buf.at[step, g]
                pltpu.make_async_copy(here, here, recv_c.at[h]).wait()

        attended = base_scr[step] + mm3(reach_scr[step], in_buf[step])
        scale = lax.rsqrt(jnp.mean(attended * attended, axis=-1, keepdims=True) + 1e-6)
        got = (attended * scale * gain).astype(BF16)
        for g in range(GROUP):
            normed[:, head_cols(step + pairs * g)] = got[g]
        return 0

    lax.fori_loop(0, pairs, attend, 0)

    def push(src, dst, kind, c, recv, where):
        return pltpu.make_async_remote_copy(
            src_ref=src, dst_ref=dst, send_sem=send_sem.at[c, kind], recv_sem=recv,
            device_id=(seq, where), device_id_type=MESH,
        )

    def far_a(c):
        return push(part.at[c, 0, far], relay.at[c, 0], 0, c, relay_sem.at[c, 0], right)

    def far_b(c):
        return push(part.at[c, 1, far], relay.at[c, 1], 1, c, relay_sem.at[c, 1], left)

    def near_b(c):
        return push(part.at[c, 1, right], landed.at[c, 1], 2, c, land_sem.at[c, 1], right)

    def near_a(c):
        return push(part.at[c, 0, left], landed.at[c, 2], 3, c, land_sem.at[c, 2], left)

    def sum_a(c):
        return push(part.at[c, 0, right], landed.at[c, 0], 4, c, land_sem.at[c, 0], right)

    def sum_b(c):
        return push(part.at[c, 1, left], landed.at[c, 3], 5, c, land_sem.at[c, 3], left)

    def merge(c):
        far_a(c).wait_recv()
        part[c, 0, right] = part[c, 0, right] + relay[c, 0]
        sum_a(c).start()
        far_b(c).wait_recv()
        part[c, 1, left] = part[c, 1, left] + relay[c, 1]
        sum_b(c).start()
        return 0

    def compute(c):
        load(c).wait()
        got = lax.dot_general(
            normed[...], w_buf[c], (((1,), (0,)), ((), ())), preferred_element_type=F32
        )
        part[c, 0] = got[:, :half].reshape(ring, rows, half)
        part[c, 1] = got[:, half:].reshape(ring, rows, half)
        far_a(c).start()
        far_b(c).start()
        return 0

    lax.fori_loop(0, chunks, lambda c, _: compute(c), 0)

    def near(c, _):
        near_b(c).start()
        near_a(c).start()
        return 0

    lax.fori_loop(0, chunks, near, 0)
    lax.fori_loop(0, chunks, lambda c, _: merge(c), 0)

    @pl.when(at_end)
    def _():
        for offset in range(1, heads):
            other = lax.rem(i + offset, heads)
            pltpu.make_async_copy(finals.at[other], finals.at[other], share_recv.at[other]).wait()
        for plane in range(planes):
            picked = owned(plane * heads + i)
            total = finals[0] * picked[:, 0:1]
            for h in range(1, heads):
                total = total + finals[h] * picked[:, h:h + 1]
            if plane < planes - 1:
                chosen[plane] = total
                give(plane).start()
            else:
                taken[...] = total

    def finish(c, _):
        for copy in (sum_a(c), near_b(c), near_a(c), sum_b(c)):
            copy.wait_recv()
        one = part[c, 0, me] + landed[c, 0] + landed[c, 2]
        two = part[c, 1, me] + landed[c, 1] + landed[c, 3]
        out_ref[:, pl.ds(pl.multiple_of(c * width, width), width)] = jnp.concatenate(
            [one, two], axis=1
        ).astype(out_ref.dtype)
        for copy in (far_a(c), far_b(c), near_b(c), near_a(c), sum_a(c), sum_b(c)):
            copy.wait_send()
        return 0

    lax.fori_loop(0, chunks, finish, 0)

    @pl.when(at_end)
    def _():
        for offset in range(1, heads):
            share(offset).wait_send()
        for plane in range(planes - 1):
            give(plane).wait_send()

    @pl.when(z != planes - 1)
    def _():
        give(0).wait_recv()

    mine = owned(seq)
    for h in range(heads):
        states_ref[0, h] = taken[...] * mine[:, h:h + 1]

    for offset in range(1, heads):
        give_a(peer(offset)).wait_send()
        give_c(offset).wait_send()
    for p in range(PIECES):
        for s in range(n_up):
            hop(s, p, True).wait_send()
        for s in range(n_dn):
            hop(s, p, False).wait_send()


def whole(queries, keys, vals, small, out_weight, heads, planes, ring, chunks=8):
    tokens, wide = queries.shape
    nb = tokens // TB
    depth, columns = out_weight.shape
    width = columns // chunks
    rows, half = tokens // ring, width // 2
    n_up, n_dn = planes // 2, planes - 1 - planes // 2
    dma = pltpu.SemaphoreType.DMA
    vmem = pl.BlockSpec(memory_space=pltpu.VMEM)
    outside = pl.BlockSpec(memory_space=pl.ANY)
    hbm = pl.BlockSpec(memory_space=pltpu.HBM)
    pair = (heads, K, 2 * K)
    return pl.pallas_call(
        functools.partial(whole_kernel, planes),
        in_specs=[hbm, outside, outside, vmem, hbm],
        out_specs=[vmem, vmem],
        out_shape=[
            jax.ShapeDtypeStruct((rows, columns), BF16),
            jax.ShapeDtypeStruct((1, heads, K, K), F32),
        ],
        scratch_shapes=[
            pltpu.VMEM((K, K), F32),
            pltpu.VMEM((heads // GROUP, 2, tokens, GROUP * K), BF16),
            pltpu.VMEM((heads // GROUP, 2, tokens, GROUP * K), BF16),
            pltpu.VMEM((tokens, wide), BF16),
            pltpu.VMEM((chunks, depth, width), BF16),
            pltpu.VMEM((tokens, 9 * heads), BF16),
            pltpu.VMEM((heads, nb * ROWS), F32),
            pltpu.VMEM(pair, F32),
            pltpu.VMEM(pair, F32),
            pltpu.VMEM((heads // GROUP, GROUP * nb, ROWS, 2 * K), BF16),
            pltpu.VMEM((heads // GROUP, GROUP * nb, ROWS, 2 * K), BF16),
            pltpu.VMEM((heads // GROUP, GROUP * nb, K, ROWS), BF16),
            pltpu.VMEM((heads // GROUP, GROUP * nb, K, ROWS), BF16),
            pltpu.VMEM((heads // GROUP, nb - 1, GROUP, K, 2 * K), F32),
            pltpu.VMEM((heads // GROUP, GROUP, tokens, K), F32),
            pltpu.VMEM((heads // GROUP, GROUP, tokens, K), F32),
            pltpu.VMEM((n_up, K, 2 * K), F32),
            pltpu.VMEM((n_dn, K, 2 * K), F32),
            pltpu.VMEM((heads, K, K), F32),
            pltpu.VMEM((heads // GROUP, GROUP, K, K), F32),
            pltpu.VMEM((K, K), F32),
            pltpu.VMEM((tokens, depth), BF16),
            pltpu.VMEM((chunks, 2, ring, rows, half), F32),
            pltpu.VMEM((chunks, 2, rows, half), F32),
            pltpu.VMEM((chunks, 4, rows, half), F32),
            pltpu.VMEM((heads, K, K), F32),
            pltpu.VMEM((planes - 1, K, K), F32),
            dma((1,)), dma((heads // GROUP, GROUP, 2)), dma((chunks,)), dma((heads - 1,)), dma((heads,)),
            dma((n_up, PIECES)), dma((n_up, PIECES)), dma((n_dn, PIECES)), dma((n_dn, PIECES)),
            dma((heads - 1,)), dma((heads,)),
            dma((chunks, 6)), dma((chunks, 2)), dma((chunks, 4)),
            dma((heads - 1,)), dma((heads,)), dma((planes - 1,)), dma((1,)),
        ],
        compiler_params=pltpu.CompilerParams(
            collective_id=1, has_side_effects=True, vmem_limit_bytes=50 * 1024 * 1024
        ),
        name="whole",
    )(queries, keys, vals, small, out_weight)


def per_device(
    queries, key_vectors, values, beta_rates, log_gate, norm_gain, out_weight, decode_owner
):
    heads = log_gate.shape[1]
    planes = lax.axis_size("seq") // heads
    tokens = queries.shape[0]
    small = jnp.concatenate(
        [
            log_gate.T, beta_rates.T,
            jnp.pad(norm_gain.reshape(1, K), ((0, 0), (0, tokens - K))),
            jnp.pad(decode_owner.astype(F32), ((0, 0), (0, tokens - heads))),
            jnp.zeros((5, tokens), F32),
        ],
        axis=0,
    )
    return whole(
        queries, key_vectors.transpose(1, 0, 2), values.transpose(1, 0, 2), small, out_weight,
        heads, planes, lax.axis_size("head"),
    )


def solution(mesh):
    in_specs = (
        P("seq", "head"), P("seq", None, "head"), P("seq", None, "head"), P("seq", "head"),
        P("seq", "head"), P(), P("head", None), P(None, "head"),
    )
    out_specs = (P(("seq", "head"), None), P("seq", "head", None, None))
    return jax.shard_map(
        per_device, mesh=mesh, in_specs=in_specs, out_specs=out_specs, check_vma=False
    )
```

```python
import functools
import jax
import jax.numpy as jnp
from jax import lax
from jax.experimental import pallas as pl
from jax.experimental.pallas import tpu as pltpu
from jax.sharding import PartitionSpec as P

K = 128
TB = 64
ROWS = 2 * TB
SUB = 8
F32 = jnp.float32
BF16 = jnp.bfloat16


def split(x):
    hi = x.astype(BF16)
    return hi, (x - hi.astype(F32)).astype(BF16)


def bdot(a, b):
    if a.ndim == 2:
        return lax.dot_general(a, b, (((1,), (0,)), ((), ())), preferred_element_type=F32)
    return lax.dot_general(a, b, (((2,), (1,)), ((0,), (0,))), preferred_element_type=F32)


def mm3(a, b):
    ah, al = a if isinstance(a, tuple) else split(a)
    bh, bl = b if isinstance(b, tuple) else split(b)
    wide = jnp.concatenate([ah, al, ah], axis=-1)
    tall = jnp.concatenate([bh, bh, bl], axis=-2)
    return bdot(wide, tall)


def twin(a, b):
    n, m, k = a.shape
    ah, al = split(a)
    bh, bl = b if isinstance(b, tuple) else split(b)
    wide = jnp.concatenate([ah, al, ah], axis=-1).reshape(n // 2, 2 * m, 3 * k)
    bh, bl = [jnp.concatenate([x.reshape(n // 2, 2, k, k)[:, t] for t in range(2)], axis=-1) for x in (bh, bl)]
    got = bdot(wide, jnp.concatenate([bh, bh, bl], axis=-2))
    return jnp.stack([got[:, :m, :k], got[:, m:, k:]], axis=1).reshape(n, m, k)


def iota(shape, dim):
    return lax.broadcasted_iota(jnp.int32, shape, dim)


MESH = pl.DeviceIdType.MESH
PIECES = 2
GROUP = 4


def place(wide_c):
    return jnp.concatenate([wide_c, jnp.zeros(wide_c.shape, F32)], axis=-1)


def masks():
    r_i, s_i = iota((ROWS, ROWS), 0), iota((ROWS, ROWS), 1)
    return r_i, s_i, r_i % TB, s_i % TB


def decays(run, run_lane):
    seen = iota((TB, ROWS), 1) % TB <= iota((TB, ROWS), 0)
    return jnp.where(seen, jnp.exp(jnp.where(seen, run - run_lane, 0.0)), 0.0)


def odd_rows(x, size, which=1):
    groups = x.reshape(x.shape[0], ROWS // (2 * size), 2, size, x.shape[-1])
    return groups[:, :, which].reshape(x.shape[0], ROWS // 2, x.shape[-1])


def among_odd(odd, even, size):
    shape = (odd.shape[0], ROWS // (2 * size), 1, size, odd.shape[-1])
    both = jnp.concatenate([even.reshape(shape), odd.reshape(shape)], axis=2)
    return both.reshape(odd.shape[0], ROWS, odd.shape[-1])


def three(x):
    one = x.astype(BF16).astype(F32)
    two = (x - one).astype(BF16).astype(F32)
    return [one, two, x - one - two]


def invert(system, nb, r_t, s_t):
    near = (r_t // SUB) == (s_t // SUB)
    folded = jnp.sum(
        jnp.where(near, system, 0.0).reshape(nb, 2, TB // SUB, SUB, ROWS), axis=2
    ).reshape(nb * 2 * SUB, ROWS)
    e_i, e_l = iota((2 * SUB, ROWS), 0), iota((2 * SUB, ROWS), 1)
    eye = jnp.where(((e_i // SUB) == (e_l // TB)) & ((e_i % SUB) == (e_l % SUB)), 1.0, 0.0).astype(F32)
    inv = jnp.broadcast_to(eye, (nb, 2 * SUB, ROWS))
    base = (iota((nb * 2 * SUB, ROWS), 1) % TB) // SUB * SUB
    for i in range(SUB):
        for j in range(2):
            if i == SUB - 1 and j == 1:
                continue
            factor = jnp.take_along_axis(folded, base + (j * TB + i), axis=1, mode="promise_in_bounds")
            factor = factor.reshape(nb, 2 * SUB, ROWS)
            at = j * SUB + i
            inv = inv - factor * inv[:, at:at + 1, :]
    solve = jnp.broadcast_to(
        inv.reshape(nb, 2, 1, SUB, ROWS), (nb, 2, TB // SUB, SUB, ROWS)
    ).reshape(nb, ROWS, ROWS)
    solve = jnp.where(near, solve, 0.0)
    size = SUB
    while size < TB:
        pair = ((r_t // (2 * size)) == (s_t // (2 * size))) & ((r_t // size) > (s_t // size))
        later = odd_rows(solve, size)
        crossed = twin(odd_rows(jnp.where(pair, system, 0.0), size), solve)
        later = later - twin(later, among_odd(crossed, jnp.zeros_like(crossed), size))
        solve = among_odd(later, odd_rows(solve, size, 0), size)
        size *= 2
    return solve


def whole_kernel(
    planes, q_buf, k_ref, v_ref, small_ref, w_ref,
    out_ref, states_ref, taken, w_buf, col_scr, row_scr, sp, total_buf, gath, rows_hi, rows_lo,
    kt_hi, kt_lo, carry, reach_scr, base_scr, from_low, from_high, out_buf, in_buf, end_buf,
    normed, part, relay, landed, finals, chosen,
    w_sem, send_a, recv_a, send_up, recv_up, send_dn, recv_dn, send_c, recv_c,
    send_sem, relay_sem, land_sem, share_send, share_recv, give_send, give_recv,
):
    tokens = small_ref.shape[1]
    heads = sp.shape[0]
    nb = tokens // TB
    chunks, depth, width = w_buf.shape
    half = width // 2
    ring = part.shape[2]
    rows = tokens // ring
    seq, me = lax.axis_index("seq"), lax.axis_index("head")
    z, i = seq // heads, lax.rem(seq, heads)
    at_end = z == planes - 1
    up = (lax.rem(z + 1, planes) * heads + i, me)
    down = (lax.rem(z + planes - 1, planes) * heads + i, me)
    n_up, n_dn = from_low.shape[0], from_high.shape[0]
    right, left = lax.rem(me + 1, ring), lax.rem(me + ring - 1, ring)
    far = lax.rem(me + 2, ring)

    def peer(offset):
        return lax.rem(i + offset, heads)

    def load(c):
        return pltpu.make_async_copy(w_ref.at[:, pl.ds(c * width, width)], w_buf.at[c], w_sem.at[c])

    pairs = heads // GROUP

    for c in range(chunks):
        load(c).start()

    barrier = pltpu.get_barrier_semaphore()
    for offset in range(1, heads):
        pl.semaphore_signal(barrier, inc=1, device_id=(z * heads + peer(offset), me), device_id_type=MESH)
    for where in (up, down, (seq, right), (seq, left)):
        pl.semaphore_signal(barrier, inc=1, device_id=where, device_id_type=MESH)

    @pl.when(z != planes - 1)
    def _():
        source = (planes - 1) * heads + i
        pl.semaphore_signal(barrier, inc=1, device_id=(source, me), device_id_type=MESH)

    gate = small_ref[0:heads]
    t_i, s_i = iota((tokens, tokens), 0), iota((tokens, tokens), 1)
    upto = jnp.where(((t_i // TB) == (s_i // TB)) & (s_i <= t_i), 1.0, 0.0).astype(F32)
    run = lax.dot_general(
        gate, upto, (((1,), (1,)), ((), ())), precision=lax.Precision.HIGHEST, preferred_element_type=F32
    )
    terms = jnp.concatenate(three(small_ref[heads:3 * heads]) + three(run), axis=0).astype(BF16)
    same = jnp.where(t_i == s_i, 1.0, 0.0).astype(BF16)
    col_scr[...] = lax.dot_general(
        same, terms, (((1,), (1,)), ((), ())), preferred_element_type=F32
    ).astype(BF16)
    row_scr[...] = jnp.concatenate(
        [run[:, b // 2 * TB:(b // 2 + 1) * TB] for b in range(2 * nb)], axis=1
    )

    batch = GROUP * nb

    def columns(h0, kinds):
        shape = (9 * heads, K)
        at = iota(shape, 0)
        rate_at, run_at = jnp.where(at < 6 * heads, at % (2 * heads), -1), jnp.where(at < 6 * heads, -1, at % heads)
        picks = []
        for kind in kinds:
            for g in range(GROUP):
                hit = (run_at == h0 + pairs * g) if kind == 2 else (rate_at == 2 * (h0 + pairs * g) + kind)
                picks.append(jnp.where(hit, 1.0, 0.0).astype(BF16))
        got = lax.dot_general(
            col_scr[...], jnp.concatenate(picks, axis=1), (((1,), (0,)), ((), ())), preferred_element_type=F32
        )
        tiles = [got[:, n * K:(n + 1) * K].reshape(nb, TB, K) for n in range(len(picks))]
        return [jnp.concatenate(tiles[n:n + GROUP], axis=0) for n in range(0, len(picks), GROUP)]

    def lane_rows(h0):
        got = []
        for g in range(GROUP):
            picked = jnp.sum(
                jnp.where(iota((heads, nb * ROWS), 0) == h0 + pairs * g, row_scr[...], 0.0), axis=0, keepdims=True
            )
            got += [picked[:, b * ROWS:(b + 1) * ROWS] for b in range(nb)]
        return jnp.stack(got, axis=0)

    def head_cols(h):
        return pl.ds(pl.multiple_of(h * K, K), K)

    def by_head(ref, h0):
        return jnp.concatenate(
            [ref[:, head_cols(h0 + pairs * g)].astype(F32).reshape(nb, TB, K) for g in range(GROUP)], axis=0
        )

    def unit(x):
        return x * lax.rsqrt(jnp.sum(x * x, axis=-1, keepdims=True) + 1e-6)

    def give_a(h):
        where = jnp.where(h > i, h - 1, h)
        return pltpu.make_async_remote_copy(
            src_ref=sp.at[h], dst_ref=gath.at[i], send_sem=send_a.at[where],
            recv_sem=recv_a.at[i], device_id=(z * heads + h, me), device_id_type=MESH,
        )

    def transition(step, _):
        pair = h0 = step
        rate0, rate1, run = columns(h0, (0, 1, 2))
        run_lane = lane_rows(h0)
        closing = run_lane[:, :, ROWS - 1:ROWS]
        rates = jnp.concatenate([rate0, rate1], axis=1)
        key = unit(jnp.concatenate([by_head(k_ref.at[j], h0) for j in range(2)], axis=1))
        val = jnp.concatenate([by_head(v_ref.at[j], h0) for j in range(2)], axis=1)
        key_t = jnp.stack([key[b].T for b in range(batch)], axis=0)
        kth, ktl = split(key_t)
        kt_hi[pair], kt_lo[pair] = kth, ktl
        decay = decays(run, run_lane)
        r_i, s_i, r_t, s_t = masks()
        below = (r_t > s_t) | ((r_t == s_t) & (r_i > s_i))
        gram = twin(key, (kth, ktl))
        system = jnp.where(below, rates * jnp.concatenate([decay, decay], axis=1) * gram, 0.0)
        solve = invert(system, batch, r_t, s_t)
        grown = jnp.exp(jnp.concatenate([run, run], axis=1))
        got = split(mm3(solve, jnp.concatenate([rates * val, (rates * grown) * key], axis=2)))
        rows_hi[pair], rows_lo[pair] = got
        z_rows = mm3(key_t * jnp.exp(closing - run_lane), got)
        k_i, k_j = iota((K, K), 0), iota((K, K), 1)
        ident = jnp.where(k_i == k_j, 1.0, 0.0).astype(F32)
        move = (jnp.exp(closing) * ident - z_rows[:, :, K:]).reshape(GROUP, nb, K, K)
        fresh = z_rows[:, :, :K].reshape(GROUP, nb, K, K)
        state = jnp.concatenate([fresh[:, 0], move[:, 0]], axis=2)
        for b in range(1, nb):
            carry[pair, b - 1] = state
            state = mm3(move[:, b], state) + place(fresh[:, b])
        for g in range(GROUP):
            sp[h0 + pairs * g] = state[g]

        @pl.when((step == 0) & at_end)
        def _():
            pl.semaphore_wait(barrier, heads + 3 + planes - 1)

        @pl.when((step == 0) & (z != planes - 1))
        def _():
            pl.semaphore_wait(barrier, heads + 3)

        for g in range(GROUP):
            @pl.when(h0 + pairs * g != i)
            def _():
                give_a(h0 + pairs * g).start()

            @pl.when(h0 + pairs * g == i)
            def _():
                gath[i] = state[g]

        return 0

    lax.fori_loop(0, pairs, transition, 0)

    def reaches(pair, _):
        h0 = pair
        (run,) = columns(h0, (2,))
        query = by_head(q_buf, h0)
        scores = mm3(query, (kt_hi[pair], kt_lo[pair])) * decays(run, lane_rows(h0))
        z_out = mm3(scores, (rows_hi[pair], rows_lo[pair])).reshape(GROUP, nb, TB, 2 * K)
        reach = (jnp.exp(run) * query).reshape(GROUP, nb, TB, K) - z_out[..., K:]
        base = [z_out[:, 0, :, :K]]
        whole_reach = [reach[:, 0]]
        for b in range(1, nb):
            both = mm3(reach[:, b], carry[pair, b - 1])
            base.append(both[:, :, :K] + z_out[:, b, :, :K])
            whole_reach.append(both[:, :, K:])
        base_scr[pair] = jnp.concatenate(base, axis=1)
        reach_scr[pair] = jnp.concatenate(whole_reach, axis=1)
        return 0

    early = jnp.where(lax.rem(i, pairs) == 0, 0, pairs)
    lax.fori_loop(0, early, reaches, 0)
    for src in range(heads):
        @pl.when(src != i)
        def _():
            pltpu.make_async_copy(gath.at[src], gath.at[src], recv_a.at[src]).wait()
    def compose(later, earlier):
        return mm3(later[..., K:], earlier) + place(later[..., :K])

    odd = gath[1], gath[3], gath[5], gath[7]
    twos = compose(jnp.stack(odd), jnp.stack([gath[0], gath[2], gath[4], gath[6]]))
    fours = compose(jnp.stack([twos[1], twos[3]]), jnp.stack([twos[0], twos[2]]))
    total_buf[...] = compose(fours[1], fours[0])

    bit = K // PIECES

    def hop(s, p, upward):
        slots = from_low if upward else from_high
        src = total_buf if s == 0 else slots.at[s - 1]
        send, recv = (send_up, recv_up) if upward else (send_dn, recv_dn)
        lines = pl.ds(p * bit, bit)
        return pltpu.make_async_remote_copy(
            src_ref=src.at[lines], dst_ref=slots.at[s, lines], send_sem=send.at[s, p],
            recv_sem=recv.at[s, p], device_id=up if upward else down, device_id_type=MESH,
        )

    for p in range(PIECES):
        hop(0, p, True).start()
        hop(0, p, False).start()
    firsts = compose(jnp.stack([gath[2], gath[4], twos[2]]), jnp.stack([twos[0], fours[0], fours[0]]))
    gath[6] = compose(gath[6], firsts[2])
    gath[1], gath[3] = twos[0], fours[0]
    gath[2], gath[4], gath[5] = firsts[0], firsts[1], firsts[2]
    gath[7] = total_buf[...]
    k_i, k_j = iota((K, 2 * K), 0), iota((K, 2 * K), 1)
    acc = jnp.where(k_i + K == k_j, 1.0, 0.0).astype(F32)
    state = jnp.zeros((K, K), F32)
    for s in range(n_up):
        if s == 0:
            lax.fori_loop(early, pairs, reaches, 0)
        if s == n_up - 1:
            prefix = gath[...]
            near = mm3(prefix[:, :, K:].reshape(heads * K, K), acc).reshape(heads, K, 2 * K)
            ready = jnp.concatenate([acc[None], near + place(prefix[:, :, :K])], axis=0)
        for p in range(PIECES):
            hop(s, p, True).wait_recv()
            if s + 1 < n_up:
                hop(s + 1, p, True).start()
            if s < n_dn:
                hop(s, p, False).wait_recv()
                if s + 1 < n_dn:
                    hop(s + 1, p, False).start()
        earlier = from_low[s]
        if s == n_up - 1:
            moved = mm3(earlier[:, K:], state) + earlier[:, :K]
            state = jnp.where(z >= n_up, moved, state)
            break
        joined = earlier if s == 0 else mm3(acc[:, K:], earlier) + place(acc[:, :K])
        acc = jnp.where(z >= s + 1, joined, acc)
        if s < n_dn:
            wrapped = from_high[s]
            moved = wrapped[:, :K] if s == 0 else mm3(wrapped[:, K:], state) + wrapped[:, :K]
            state = jnp.where(z + s + 1 >= planes, moved, state)
    spread_out = mm3(ready[:, :, K:].reshape((heads + 1) * K, K), state).reshape(heads + 1, K, K)
    spread_out = spread_out + ready[:, :, :K]
    out_buf[...] = spread_out[:heads]
    end_buf[...] = spread_out[heads]

    def give_c(offset):
        other = peer(offset)
        return pltpu.make_async_remote_copy(
            src_ref=out_buf.at[other], dst_ref=in_buf.at[lax.rem(i, pairs), i // pairs], send_sem=send_c.at[offset - 1],
            recv_sem=recv_c.at[i], device_id=(z * heads + other, me), device_id_type=MESH,
        )

    def share(offset):
        other = peer(offset)
        return pltpu.make_async_remote_copy(
            src_ref=end_buf, dst_ref=finals.at[i], send_sem=share_send.at[offset - 1],
            recv_sem=share_recv.at[i], device_id=(z * heads + other, me), device_id_type=MESH,
        )

    def give(plane):
        return pltpu.make_async_remote_copy(
            src_ref=chosen.at[plane], dst_ref=taken, send_sem=give_send.at[plane],
            recv_sem=give_recv.at[0], device_id=(plane * heads + i, me), device_id_type=MESH,
        )

    for offset in range(1, heads):
        give_c(offset).start()
    in_buf[lax.rem(i, pairs), i // pairs] = out_buf[i]

    @pl.when(at_end)
    def _():
        finals[i] = end_buf[...]
        for offset in range(1, heads):
            share(offset).start()

    gain = small_ref[3 * heads:3 * heads + 1, 0:K]

    def owned(device):
        owners = small_ref[3 * heads + 1:3 * heads + 3, 0:heads]
        found = jnp.where(owners == lax.convert_element_type(device, F32), 1.0, 0.0).astype(F32)
        return jnp.max(found, axis=0, keepdims=True)


    def attend(step, _):
        for g in range(GROUP):
            h = step + pairs * g

            @pl.when(h != i)
            def _():
                here = in_buf.at[step, g]
                pltpu.make_async_copy(here, here, recv_c.at[h]).wait()

        attended = base_scr[step] + mm3(reach_scr[step], in_buf[step])
        scale = lax.rsqrt(jnp.mean(attended * attended, axis=-1, keepdims=True) + 1e-6)
        got = (attended * scale * gain).astype(BF16)
        for g in range(GROUP):
            normed[:, head_cols(step + pairs * g)] = got[g]
        return 0

    lax.fori_loop(0, pairs, attend, 0)

    def push(src, dst, kind, c, recv, where):
        return pltpu.make_async_remote_copy(
            src_ref=src, dst_ref=dst, send_sem=send_sem.at[c, kind], recv_sem=recv,
            device_id=(seq, where), device_id_type=MESH,
        )

    def far_a(c):
        return push(part.at[c, 0, far], relay.at[c, 0], 0, c, relay_sem.at[c, 0], right)

    def far_b(c):
        return push(part.at[c, 1, far], relay.at[c, 1], 1, c, relay_sem.at[c, 1], left)

    def near_b(c):
        return push(part.at[c, 1, right], landed.at[c, 1], 2, c, land_sem.at[c, 1], right)

    def near_a(c):
        return push(part.at[c, 0, left], landed.at[c, 2], 3, c, land_sem.at[c, 2], left)

    def sum_a(c):
        return push(part.at[c, 0, right], landed.at[c, 0], 4, c, land_sem.at[c, 0], right)

    def sum_b(c):
        return push(part.at[c, 1, left], landed.at[c, 3], 5, c, land_sem.at[c, 3], left)

    def merge(c):
        far_a(c).wait_recv()
        part[c, 0, right] = part[c, 0, right] + relay[c, 0]
        sum_a(c).start()
        far_b(c).wait_recv()
        part[c, 1, left] = part[c, 1, left] + relay[c, 1]
        sum_b(c).start()
        return 0

    def compute(c):
        load(c).wait()
        got = lax.dot_general(
            normed[...], w_buf[c], (((1,), (0,)), ((), ())), preferred_element_type=F32
        )
        part[c, 0] = got[:, :half].reshape(ring, rows, half)
        part[c, 1] = got[:, half:].reshape(ring, rows, half)
        far_a(c).start()
        far_b(c).start()
        return 0

    lax.fori_loop(0, chunks, lambda c, _: compute(c), 0)

    def near(c, _):
        near_b(c).start()
        near_a(c).start()
        return 0

    lax.fori_loop(0, chunks, near, 0)
    lax.fori_loop(0, chunks, lambda c, _: merge(c), 0)

    @pl.when(at_end)
    def _():
        for offset in range(1, heads):
            other = lax.rem(i + offset, heads)
            pltpu.make_async_copy(finals.at[other], finals.at[other], share_recv.at[other]).wait()
        for plane in range(planes):
            picked = owned(plane * heads + i)
            total = finals[0] * picked[:, 0:1]
            for h in range(1, heads):
                total = total + finals[h] * picked[:, h:h + 1]
            if plane < planes - 1:
                chosen[plane] = total
                give(plane).start()
            else:
                taken[...] = total

    def finish(c, _):
        for copy in (sum_a(c), near_b(c), near_a(c), sum_b(c)):
            copy.wait_recv()
        one = part[c, 0, me] + landed[c, 0] + landed[c, 2]
        two = part[c, 1, me] + landed[c, 1] + landed[c, 3]
        out_ref[:, pl.ds(pl.multiple_of(c * width, width), width)] = jnp.concatenate(
            [one, two], axis=1
        ).astype(out_ref.dtype)
        for copy in (far_a(c), far_b(c), near_b(c), near_a(c), sum_a(c), sum_b(c)):
            copy.wait_send()
        return 0

    lax.fori_loop(0, chunks, finish, 0)

    @pl.when(at_end)
    def _():
        for offset in range(1, heads):
            share(offset).wait_send()
        for plane in range(planes - 1):
            give(plane).wait_send()

    @pl.when(z != planes - 1)
    def _():
        give(0).wait_recv()

    mine = owned(seq)
    for h in range(heads):
        states_ref[0, h] = taken[...] * mine[:, h:h + 1]

    for offset in range(1, heads):
        give_a(peer(offset)).wait_send()
        give_c(offset).wait_send()
    for p in range(PIECES):
        for s in range(n_up):
            hop(s, p, True).wait_send()
        for s in range(n_dn):
            hop(s, p, False).wait_send()


def whole(queries, keys, vals, small, out_weight, heads, planes, ring, chunks=8):
    tokens, wide = queries.shape
    nb = tokens // TB
    depth, columns = out_weight.shape
    width = columns // chunks
    rows, half = tokens // ring, width // 2
    n_up, n_dn = planes // 2, planes - 1 - planes // 2
    dma = pltpu.SemaphoreType.DMA
    vmem = pl.BlockSpec(memory_space=pltpu.VMEM)
    hbm = pl.BlockSpec(memory_space=pltpu.HBM)
    pair = (heads, K, 2 * K)
    return pl.pallas_call(
        functools.partial(whole_kernel, planes),
        in_specs=[vmem, vmem, vmem, vmem, hbm],
        out_specs=[vmem, vmem],
        out_shape=[
            jax.ShapeDtypeStruct((rows, columns), BF16),
            jax.ShapeDtypeStruct((1, heads, K, K), F32),
        ],
        scratch_shapes=[
            pltpu.VMEM((K, K), F32),
            pltpu.VMEM((chunks, depth, width), BF16),
            pltpu.VMEM((tokens, 9 * heads), BF16),
            pltpu.VMEM((heads, nb * ROWS), F32),
            pltpu.VMEM(pair, F32),
            pltpu.VMEM((K, 2 * K), F32),
            pltpu.VMEM(pair, F32),
            pltpu.VMEM((heads // GROUP, GROUP * nb, ROWS, 2 * K), BF16),
            pltpu.VMEM((heads // GROUP, GROUP * nb, ROWS, 2 * K), BF16),
            pltpu.VMEM((heads // GROUP, GROUP * nb, K, ROWS), BF16),
            pltpu.VMEM((heads // GROUP, GROUP * nb, K, ROWS), BF16),
            pltpu.VMEM((heads // GROUP, nb - 1, GROUP, K, 2 * K), F32),
            pltpu.VMEM((heads // GROUP, GROUP, tokens, K), F32),
            pltpu.VMEM((heads // GROUP, GROUP, tokens, K), F32),
            pltpu.VMEM((n_up, K, 2 * K), F32),
            pltpu.VMEM((n_dn, K, 2 * K), F32),
            pltpu.VMEM((heads, K, K), F32),
            pltpu.VMEM((heads // GROUP, GROUP, K, K), F32),
            pltpu.VMEM((K, K), F32),
            pltpu.VMEM((tokens, depth), BF16),
            pltpu.VMEM((chunks, 2, ring, rows, half), F32),
            pltpu.VMEM((chunks, 2, rows, half), F32),
            pltpu.VMEM((chunks, 4, rows, half), F32),
            pltpu.VMEM((heads, K, K), F32),
            pltpu.VMEM((planes - 1, K, K), F32),
            dma((chunks,)), dma((heads - 1,)), dma((heads,)),
            dma((n_up, PIECES)), dma((n_up, PIECES)), dma((n_dn, PIECES)), dma((n_dn, PIECES)),
            dma((heads - 1,)), dma((heads,)),
            dma((chunks, 6)), dma((chunks, 2)), dma((chunks, 4)),
            dma((heads - 1,)), dma((heads,)), dma((planes - 1,)), dma((1,)),
        ],
        compiler_params=pltpu.CompilerParams(
            collective_id=1, has_side_effects=True, vmem_limit_bytes=50 * 1024 * 1024
        ),
        name="whole",
    )(queries, keys, vals, small, out_weight)


def per_device(
    queries, key_vectors, values, beta_rates, log_gate, norm_gain, out_weight, decode_owner
):
    heads = log_gate.shape[1]
    planes = lax.axis_size("seq") // heads
    tokens = queries.shape[0]
    lines = 4 * heads

    def laid(x, first):
        return jnp.pad(x, ((first, lines - first - x.shape[0]), (0, tokens - x.shape[1])))

    small = (
        laid(log_gate.T, 0) + laid(beta_rates.T, heads) + laid(norm_gain.reshape(1, K), 3 * heads)
        + laid(decode_owner, 3 * heads + 1).astype(F32)
    )
    return whole(
        queries, key_vectors.transpose(1, 0, 2), values.transpose(1, 0, 2), small, out_weight,
        heads, planes, lax.axis_size("head"),
    )


def solution(mesh):
    in_specs = (
        P("seq", "head"), P("seq", None, "head"), P("seq", None, "head"), P("seq", "head"),
        P("seq", "head"), P(), P("head", None), P(None, "head"),
    )
    out_specs = (P(("seq", "head"), None), P("seq", "head", None, None))
    return jax.shard_map(
        per_device, mesh=mesh, in_specs=in_specs, out_specs=out_specs, check_vma=False
    )
```

```python
import functools
import jax
import jax.numpy as jnp
from jax import lax
from jax.experimental import pallas as pl
from jax.experimental.pallas import tpu as pltpu
from jax.sharding import PartitionSpec as P

K = 128
TB = 64
ROWS = 2 * TB
SUB = 8
F32 = jnp.float32
BF16 = jnp.bfloat16


def split(x):
    hi = x.astype(BF16)
    return hi, (x - hi.astype(F32)).astype(BF16)


def bdot(a, b):
    if a.ndim == 2:
        return lax.dot_general(a, b, (((1,), (0,)), ((), ())), preferred_element_type=F32)
    return lax.dot_general(a, b, (((2,), (1,)), ((0,), (0,))), preferred_element_type=F32)


def mm3(a, b):
    ah, al = a if isinstance(a, tuple) else split(a)
    bh, bl = b if isinstance(b, tuple) else split(b)
    wide = jnp.concatenate([ah, al, ah], axis=-1)
    tall = jnp.concatenate([bh, bh, bl], axis=-2)
    return bdot(wide, tall)


def twin(a, b):
    n, m, k = a.shape
    ah, al = split(a)
    bh, bl = b if isinstance(b, tuple) else split(b)
    wide = jnp.concatenate([ah, al, ah], axis=-1).reshape(n // 2, 2 * m, 3 * k)
    bh, bl = [jnp.concatenate([x.reshape(n // 2, 2, k, k)[:, t] for t in range(2)], axis=-1) for x in (bh, bl)]
    got = bdot(wide, jnp.concatenate([bh, bh, bl], axis=-2))
    return jnp.stack([got[:, :m, :k], got[:, m:, k:]], axis=1).reshape(n, m, k)


def iota(shape, dim):
    return lax.broadcasted_iota(jnp.int32, shape, dim)


MESH = pl.DeviceIdType.MESH
PIECES = 4
GROUP = 4


def place(wide_c):
    return jnp.concatenate([wide_c, jnp.zeros(wide_c.shape, F32)], axis=-1)


def masks():
    r_i, s_i = iota((ROWS, ROWS), 0), iota((ROWS, ROWS), 1)
    return r_i, s_i, r_i % TB, s_i % TB


def decays(run, run_lane):
    seen = iota((TB, ROWS), 1) % TB <= iota((TB, ROWS), 0)
    return jnp.where(seen, jnp.exp(jnp.where(seen, run - run_lane, 0.0)), 0.0)


def odd_rows(x, size, which=1):
    groups = x.reshape(x.shape[0], ROWS // (2 * size), 2, size, x.shape[-1])
    return groups[:, :, which].reshape(x.shape[0], ROWS // 2, x.shape[-1])


def among_odd(odd, even, size):
    shape = (odd.shape[0], ROWS // (2 * size), 1, size, odd.shape[-1])
    both = jnp.concatenate([even.reshape(shape), odd.reshape(shape)], axis=2)
    return both.reshape(odd.shape[0], ROWS, odd.shape[-1])


def three(x):
    one = x.astype(BF16).astype(F32)
    two = (x - one).astype(BF16).astype(F32)
    return [one, two, x - one - two]


def invert(system, nb, r_t, s_t):
    near = (r_t // SUB) == (s_t // SUB)
    folded = jnp.sum(
        jnp.where(near, system, 0.0).reshape(nb, 2, TB // SUB, SUB, ROWS), axis=2
    ).reshape(nb * 2 * SUB, ROWS)
    e_i, e_l = iota((2 * SUB, ROWS), 0), iota((2 * SUB, ROWS), 1)
    eye = jnp.where(((e_i // SUB) == (e_l // TB)) & ((e_i % SUB) == (e_l % SUB)), 1.0, 0.0).astype(F32)
    inv = jnp.broadcast_to(eye, (nb, 2 * SUB, ROWS))
    base = (iota((nb * 2 * SUB, ROWS), 1) % TB) // SUB * SUB
    for i in range(SUB):
        for j in range(2):
            if i == SUB - 1 and j == 1:
                continue
            factor = jnp.take_along_axis(folded, base + (j * TB + i), axis=1, mode="promise_in_bounds")
            factor = factor.reshape(nb, 2 * SUB, ROWS)
            at = j * SUB + i
            inv = inv - factor * inv[:, at:at + 1, :]
    solve = jnp.broadcast_to(
        inv.reshape(nb, 2, 1, SUB, ROWS), (nb, 2, TB // SUB, SUB, ROWS)
    ).reshape(nb, ROWS, ROWS)
    solve = jnp.where(near, solve, 0.0)
    size = SUB
    while size < TB:
        pair = ((r_t // (2 * size)) == (s_t // (2 * size))) & ((r_t // size) > (s_t // size))
        later = odd_rows(solve, size)
        crossed = twin(odd_rows(jnp.where(pair, system, 0.0), size), solve)
        later = later - twin(later, among_odd(crossed, jnp.zeros_like(crossed), size))
        solve = among_odd(later, odd_rows(solve, size, 0), size)
        size *= 2
    return solve


def whole_kernel(
    planes, q_buf, k_ref, v_ref, small_ref, w_ref,
    out_ref, states_ref, taken, w_buf, col_scr, row_scr, sp, total_buf, gath, rows_hi, rows_lo,
    kt_hi, kt_lo, carry, reach_scr, base_scr, from_low, from_high, out_buf, in_buf, end_buf,
    normed, part, relay, landed, finals, chosen,
    w_sem, send_a, recv_a, send_up, recv_up, send_dn, recv_dn, send_c, recv_c,
    send_sem, relay_sem, land_sem, share_send, share_recv, give_send, give_recv,
):
    tokens = small_ref.shape[1]
    heads = sp.shape[0]
    nb = tokens // TB
    chunks, depth, width = w_buf.shape
    half = width // 2
    ring = part.shape[2]
    rows = tokens // ring
    seq, me = lax.axis_index("seq"), lax.axis_index("head")
    z, i = seq // heads, lax.rem(seq, heads)
    at_end = z == planes - 1
    up = (lax.rem(z + 1, planes) * heads + i, me)
    down = (lax.rem(z + planes - 1, planes) * heads + i, me)
    n_up, n_dn = from_low.shape[0], from_high.shape[0]
    right, left = lax.rem(me + 1, ring), lax.rem(me + ring - 1, ring)
    far = lax.rem(me + 2, ring)

    def peer(offset):
        return lax.rem(i + offset, heads)

    def load(c):
        return pltpu.make_async_copy(w_ref.at[:, pl.ds(c * width, width)], w_buf.at[c], w_sem.at[c])

    pairs = heads // GROUP

    for c in range(chunks):
        load(c).start()

    barrier = pltpu.get_barrier_semaphore()
    for offset in range(1, heads):
        pl.semaphore_signal(barrier, inc=1, device_id=(z * heads + peer(offset), me), device_id_type=MESH)
    for where in (up, down, (seq, right), (seq, left)):
        pl.semaphore_signal(barrier, inc=1, device_id=where, device_id_type=MESH)

    @pl.when(z != planes - 1)
    def _():
        source = (planes - 1) * heads + i
        pl.semaphore_signal(barrier, inc=1, device_id=(source, me), device_id_type=MESH)

    gate = small_ref[0:heads]
    t_i, s_i = iota((tokens, tokens), 0), iota((tokens, tokens), 1)
    upto = jnp.where(((t_i // TB) == (s_i // TB)) & (s_i <= t_i), 1.0, 0.0).astype(F32)
    run = lax.dot_general(
        gate, upto, (((1,), (1,)), ((), ())), precision=lax.Precision.HIGHEST, preferred_element_type=F32
    )
    terms = jnp.concatenate(three(small_ref[heads:3 * heads]) + three(run), axis=0).astype(BF16)
    same = jnp.where(t_i == s_i, 1.0, 0.0).astype(BF16)
    col_scr[...] = lax.dot_general(
        same, terms, (((1,), (1,)), ((), ())), preferred_element_type=F32
    ).astype(BF16)
    row_scr[...] = jnp.concatenate(
        [run[:, b // 2 * TB:(b // 2 + 1) * TB] for b in range(2 * nb)], axis=1
    )

    batch = GROUP * nb

    def columns(h0, kinds):
        shape = (9 * heads, K)
        at = iota(shape, 0)
        rate_at, run_at = jnp.where(at < 6 * heads, at % (2 * heads), -1), jnp.where(at < 6 * heads, -1, at % heads)
        picks = []
        for kind in kinds:
            for g in range(GROUP):
                hit = (run_at == h0 + pairs * g) if kind == 2 else (rate_at == 2 * (h0 + pairs * g) + kind)
                picks.append(jnp.where(hit, 1.0, 0.0).astype(BF16))
        got = lax.dot_general(
            col_scr[...], jnp.concatenate(picks, axis=1), (((1,), (0,)), ((), ())), preferred_element_type=F32
        )
        tiles = [got[:, n * K:(n + 1) * K].reshape(nb, TB, K) for n in range(len(picks))]
        return [jnp.concatenate(tiles[n:n + GROUP], axis=0) for n in range(0, len(picks), GROUP)]

    def lane_rows(h0):
        got = []
        for g in range(GROUP):
            picked = jnp.sum(
                jnp.where(iota((heads, nb * ROWS), 0) == h0 + pairs * g, row_scr[...], 0.0), axis=0, keepdims=True
            )
            got += [picked[:, b * ROWS:(b + 1) * ROWS] for b in range(nb)]
        return jnp.stack(got, axis=0)

    def head_cols(h):
        return pl.ds(pl.multiple_of(h * K, K), K)

    def by_head(ref, h0):
        return jnp.concatenate(
            [ref[:, head_cols(h0 + pairs * g)].astype(F32).reshape(nb, TB, K) for g in range(GROUP)], axis=0
        )

    def unit(x):
        return x * lax.rsqrt(jnp.sum(x * x, axis=-1, keepdims=True) + 1e-6)

    def give_a(h):
        where = jnp.where(h > i, h - 1, h)
        return pltpu.make_async_remote_copy(
            src_ref=sp.at[h], dst_ref=gath.at[i], send_sem=send_a.at[where],
            recv_sem=recv_a.at[i], device_id=(z * heads + h, me), device_id_type=MESH,
        )

    def transition(step, _):
        pair = h0 = step
        rate0, rate1, run = columns(h0, (0, 1, 2))
        run_lane = lane_rows(h0)
        closing = run_lane[:, :, ROWS - 1:ROWS]
        rates = jnp.concatenate([rate0, rate1], axis=1)
        key = unit(jnp.concatenate([by_head(k_ref.at[j], h0) for j in range(2)], axis=1))
        val = jnp.concatenate([by_head(v_ref.at[j], h0) for j in range(2)], axis=1)
        key_t = jnp.stack([key[b].T for b in range(batch)], axis=0)
        kth, ktl = split(key_t)
        kt_hi[pair], kt_lo[pair] = kth, ktl
        decay = decays(run, run_lane)
        r_i, s_i, r_t, s_t = masks()
        below = (r_t > s_t) | ((r_t == s_t) & (r_i > s_i))
        gram = twin(key, (kth, ktl))
        system = jnp.where(below, rates * jnp.concatenate([decay, decay], axis=1) * gram, 0.0)
        solve = invert(system, batch, r_t, s_t)
        grown = jnp.exp(jnp.concatenate([run, run], axis=1))
        got = split(mm3(solve, jnp.concatenate([rates * val, (rates * grown) * key], axis=2)))
        rows_hi[pair], rows_lo[pair] = got
        z_rows = mm3(key_t * jnp.exp(closing - run_lane), got)
        k_i, k_j = iota((K, K), 0), iota((K, K), 1)
        ident = jnp.where(k_i == k_j, 1.0, 0.0).astype(F32)
        move = (jnp.exp(closing) * ident - z_rows[:, :, K:]).reshape(GROUP, nb, K, K)
        fresh = z_rows[:, :, :K].reshape(GROUP, nb, K, K)
        state = jnp.concatenate([fresh[:, 0], move[:, 0]], axis=2)
        for b in range(1, nb):
            carry[pair, b - 1] = state
            state = mm3(move[:, b], state) + place(fresh[:, b])
        for g in range(GROUP):
            sp[h0 + pairs * g] = state[g]

        @pl.when((step == 0) & at_end)
        def _():
            pl.semaphore_wait(barrier, heads + 3 + planes - 1)

        @pl.when((step == 0) & (z != planes - 1))
        def _():
            pl.semaphore_wait(barrier, heads + 3)

        for g in range(GROUP):
            @pl.when(h0 + pairs * g != i)
            def _():
                give_a(h0 + pairs * g).start()

            @pl.when(h0 + pairs * g == i)
            def _():
                gath[i] = state[g]

        return 0

    lax.fori_loop(0, pairs, transition, 0)

    def reaches(pair, _):
        h0 = pair
        (run,) = columns(h0, (2,))
        query = by_head(q_buf, h0)
        scores = twin(query, (kt_hi[pair], kt_lo[pair])) * decays(run, lane_rows(h0))
        z_out = mm3(scores, (rows_hi[pair], rows_lo[pair])).reshape(GROUP, nb, TB, 2 * K)
        reach = (jnp.exp(run) * query).reshape(GROUP, nb, TB, K) - z_out[..., K:]
        base = [z_out[:, 0, :, :K]]
        whole_reach = [reach[:, 0]]
        for b in range(1, nb):
            both = mm3(reach[:, b], carry[pair, b - 1])
            base.append(both[:, :, :K] + z_out[:, b, :, :K])
            whole_reach.append(both[:, :, K:])
        base_scr[pair] = jnp.concatenate(base, axis=1)
        reach_scr[pair] = jnp.concatenate(whole_reach, axis=1)
        return 0

    early = jnp.where(lax.rem(i, pairs) == 0, 0, pairs)
    lax.fori_loop(0, early, reaches, 0)
    for src in range(heads):
        @pl.when(src != i)
        def _():
            pltpu.make_async_copy(gath.at[src], gath.at[src], recv_a.at[src]).wait()
    def compose(later, earlier):
        return mm3(later[..., K:], earlier) + place(later[..., :K])

    odd = gath[1], gath[3], gath[5], gath[7]
    twos = compose(jnp.stack(odd), jnp.stack([gath[0], gath[2], gath[4], gath[6]]))
    fours = compose(jnp.stack([twos[1], twos[3]]), jnp.stack([twos[0], twos[2]]))
    total_buf[...] = compose(fours[1], fours[0])

    bit = K // PIECES

    def hop(s, p, upward):
        slots = from_low if upward else from_high
        src = total_buf if s == 0 else slots.at[s - 1]
        send, recv = (send_up, recv_up) if upward else (send_dn, recv_dn)
        lines = pl.ds(p * bit, bit)
        return pltpu.make_async_remote_copy(
            src_ref=src.at[lines], dst_ref=slots.at[s, lines], send_sem=send.at[s, p],
            recv_sem=recv.at[s, p], device_id=up if upward else down, device_id_type=MESH,
        )

    for p in range(PIECES):
        hop(0, p, True).start()
        hop(0, p, False).start()
    firsts = compose(jnp.stack([gath[2], gath[4], twos[2]]), jnp.stack([twos[0], fours[0], fours[0]]))
    gath[6] = compose(gath[6], firsts[2])
    gath[1], gath[3] = twos[0], fours[0]
    gath[2], gath[4], gath[5] = firsts[0], firsts[1], firsts[2]
    gath[7] = total_buf[...]
    k_i, k_j = iota((K, 2 * K), 0), iota((K, 2 * K), 1)
    acc = jnp.where(k_i + K == k_j, 1.0, 0.0).astype(F32)
    state = jnp.zeros((K, K), F32)
    for s in range(n_up):
        if s == 0:
            lax.fori_loop(early, pairs, reaches, 0)
        if s == n_up - 1:
            prefix = gath[...]
            near = mm3(prefix[:, :, K:].reshape(heads * K, K), acc).reshape(heads, K, 2 * K)
            ready = jnp.concatenate([acc[None], near + place(prefix[:, :, :K])], axis=0)
        for p in range(PIECES):
            hop(s, p, True).wait_recv()
            if s + 1 < n_up:
                hop(s + 1, p, True).start()
            if s < n_dn:
                hop(s, p, False).wait_recv()
                if s + 1 < n_dn:
                    hop(s + 1, p, False).start()
        earlier = from_low[s]
        if s == n_up - 1:
            moved = mm3(earlier[:, K:], state) + earlier[:, :K]
            state = jnp.where(z >= n_up, moved, state)
            break
        joined = earlier if s == 0 else mm3(acc[:, K:], earlier) + place(acc[:, :K])
        acc = jnp.where(z >= s + 1, joined, acc)
        if s < n_dn:
            wrapped = from_high[s]
            moved = wrapped[:, :K] if s == 0 else mm3(wrapped[:, K:], state) + wrapped[:, :K]
            state = jnp.where(z + s + 1 >= planes, moved, state)
    spread_out = mm3(ready[:, :, K:].reshape((heads + 1) * K, K), state).reshape(heads + 1, K, K)
    spread_out = spread_out + ready[:, :, :K]
    out_buf[...] = spread_out[:heads]
    end_buf[...] = spread_out[heads]

    def give_c(offset):
        other = peer(offset)
        return pltpu.make_async_remote_copy(
            src_ref=out_buf.at[other], dst_ref=in_buf.at[lax.rem(i, pairs), i // pairs], send_sem=send_c.at[offset - 1],
            recv_sem=recv_c.at[i], device_id=(z * heads + other, me), device_id_type=MESH,
        )

    def share(offset):
        other = peer(offset)
        return pltpu.make_async_remote_copy(
            src_ref=end_buf, dst_ref=finals.at[i], send_sem=share_send.at[offset - 1],
            recv_sem=share_recv.at[i], device_id=(z * heads + other, me), device_id_type=MESH,
        )

    def give(plane):
        return pltpu.make_async_remote_copy(
            src_ref=chosen.at[plane], dst_ref=taken, send_sem=give_send.at[plane],
            recv_sem=give_recv.at[0], device_id=(plane * heads + i, me), device_id_type=MESH,
        )

    for offset in range(1, heads):
        give_c(offset).start()
    in_buf[lax.rem(i, pairs), i // pairs] = out_buf[i]

    @pl.when(at_end)
    def _():
        finals[i] = end_buf[...]
        for offset in range(1, heads):
            share(offset).start()

    gain = small_ref[3 * heads:3 * heads + 1, 0:K]

    def owned(device):
        owners = small_ref[3 * heads + 1:3 * heads + 3, 0:heads]
        found = jnp.where(owners == lax.convert_element_type(device, F32), 1.0, 0.0).astype(F32)
        return jnp.max(found, axis=0, keepdims=True)


    def attend(step, _):
        for g in range(GROUP):
            h = step + pairs * g

            @pl.when(h != i)
            def _():
                here = in_buf.at[step, g]
                pltpu.make_async_copy(here, here, recv_c.at[h]).wait()

        attended = base_scr[step] + mm3(reach_scr[step], in_buf[step])
        scale = lax.rsqrt(jnp.mean(attended * attended, axis=-1, keepdims=True) + 1e-6)
        got = (attended * scale * gain).astype(BF16)
        for g in range(GROUP):
            normed[:, head_cols(step + pairs * g)] = got[g]
        return 0

    lax.fori_loop(0, pairs, attend, 0)

    def push(src, dst, kind, c, recv, where):
        return pltpu.make_async_remote_copy(
            src_ref=src, dst_ref=dst, send_sem=send_sem.at[c, kind], recv_sem=recv,
            device_id=(seq, where), device_id_type=MESH,
        )

    def far_a(c):
        return push(part.at[c, 0, far], relay.at[c, 0], 0, c, relay_sem.at[c, 0], right)

    def far_b(c):
        return push(part.at[c, 1, far], relay.at[c, 1], 1, c, relay_sem.at[c, 1], left)

    def near_b(c):
        return push(part.at[c, 1, right], landed.at[c, 1], 2, c, land_sem.at[c, 1], right)

    def near_a(c):
        return push(part.at[c, 0, left], landed.at[c, 2], 3, c, land_sem.at[c, 2], left)

    def sum_a(c):
        return push(part.at[c, 0, right], landed.at[c, 0], 4, c, land_sem.at[c, 0], right)

    def sum_b(c):
        return push(part.at[c, 1, left], landed.at[c, 3], 5, c, land_sem.at[c, 3], left)

    def merge(c):
        far_a(c).wait_recv()
        part[c, 0, right] = part[c, 0, right] + relay[c, 0]
        sum_a(c).start()
        far_b(c).wait_recv()
        part[c, 1, left] = part[c, 1, left] + relay[c, 1]
        sum_b(c).start()
        return 0

    def compute(c):
        load(c).wait()
        got = lax.dot_general(
            normed[...], w_buf[c], (((1,), (0,)), ((), ())), preferred_element_type=F32
        )
        part[c, 0] = got[:, :half].reshape(ring, rows, half)
        part[c, 1] = got[:, half:].reshape(ring, rows, half)
        far_a(c).start()
        far_b(c).start()
        return 0

    lax.fori_loop(0, chunks, lambda c, _: compute(c), 0)

    def near(c, _):
        near_b(c).start()
        near_a(c).start()
        return 0

    lax.fori_loop(0, chunks, near, 0)
    lax.fori_loop(0, chunks, lambda c, _: merge(c), 0)

    @pl.when(at_end)
    def _():
        for offset in range(1, heads):
            other = lax.rem(i + offset, heads)
            pltpu.make_async_copy(finals.at[other], finals.at[other], share_recv.at[other]).wait()
        for plane in range(planes):
            picked = owned(plane * heads + i)
            total = finals[0] * picked[:, 0:1]
            for h in range(1, heads):
                total = total + finals[h] * picked[:, h:h + 1]
            if plane < planes - 1:
                chosen[plane] = total
                give(plane).start()
            else:
                taken[...] = total

    def finish(c, _):
        for copy in (sum_a(c), near_b(c), near_a(c), sum_b(c)):
            copy.wait_recv()
        one = part[c, 0, me] + landed[c, 0] + landed[c, 2]
        two = part[c, 1, me] + landed[c, 1] + landed[c, 3]
        out_ref[:, pl.ds(pl.multiple_of(c * width, width), width)] = jnp.concatenate(
            [one, two], axis=1
        ).astype(out_ref.dtype)
        for copy in (far_a(c), far_b(c), near_b(c), near_a(c), sum_a(c), sum_b(c)):
            copy.wait_send()
        return 0

    lax.fori_loop(0, chunks, finish, 0)

    @pl.when(at_end)
    def _():
        for offset in range(1, heads):
            share(offset).wait_send()
        for plane in range(planes - 1):
            give(plane).wait_send()

    @pl.when(z != planes - 1)
    def _():
        give(0).wait_recv()

    mine = owned(seq)
    for h in range(heads):
        states_ref[0, h] = taken[...] * mine[:, h:h + 1]

    for offset in range(1, heads):
        give_a(peer(offset)).wait_send()
        give_c(offset).wait_send()
    for p in range(PIECES):
        for s in range(n_up):
            hop(s, p, True).wait_send()
        for s in range(n_dn):
            hop(s, p, False).wait_send()


def whole(queries, keys, vals, small, out_weight, heads, planes, ring, chunks=4):
    tokens, wide = queries.shape
    nb = tokens // TB
    depth, columns = out_weight.shape
    width = columns // chunks
    rows, half = tokens // ring, width // 2
    n_up, n_dn = planes // 2, planes - 1 - planes // 2
    dma = pltpu.SemaphoreType.DMA
    vmem = pl.BlockSpec(memory_space=pltpu.VMEM)
    hbm = pl.BlockSpec(memory_space=pltpu.HBM)
    pair = (heads, K, 2 * K)
    return pl.pallas_call(
        functools.partial(whole_kernel, planes),
        in_specs=[vmem, vmem, vmem, vmem, hbm],
        out_specs=[vmem, vmem],
        out_shape=[
            jax.ShapeDtypeStruct((rows, columns), BF16),
            jax.ShapeDtypeStruct((1, heads, K, K), F32),
        ],
        scratch_shapes=[
            pltpu.VMEM((K, K), F32),
            pltpu.VMEM((chunks, depth, width), BF16),
            pltpu.VMEM((tokens, 9 * heads), BF16),
            pltpu.VMEM((heads, nb * ROWS), F32),
            pltpu.VMEM(pair, F32),
            pltpu.VMEM((K, 2 * K), F32),
            pltpu.VMEM(pair, F32),
            pltpu.VMEM((heads // GROUP, GROUP * nb, ROWS, 2 * K), BF16),
            pltpu.VMEM((heads // GROUP, GROUP * nb, ROWS, 2 * K), BF16),
            pltpu.VMEM((heads // GROUP, GROUP * nb, K, ROWS), BF16),
            pltpu.VMEM((heads // GROUP, GROUP * nb, K, ROWS), BF16),
            pltpu.VMEM((heads // GROUP, nb - 1, GROUP, K, 2 * K), F32),
            pltpu.VMEM((heads // GROUP, GROUP, tokens, K), F32),
            pltpu.VMEM((heads // GROUP, GROUP, tokens, K), F32),
            pltpu.VMEM((n_up, K, 2 * K), F32),
            pltpu.VMEM((n_dn, K, 2 * K), F32),
            pltpu.VMEM((heads, K, K), F32),
            pltpu.VMEM((heads // GROUP, GROUP, K, K), F32),
            pltpu.VMEM((K, K), F32),
            pltpu.VMEM((tokens, depth), BF16),
            pltpu.VMEM((chunks, 2, ring, rows, half), F32),
            pltpu.VMEM((chunks, 2, rows, half), F32),
            pltpu.VMEM((chunks, 4, rows, half), F32),
            pltpu.VMEM((heads, K, K), F32),
            pltpu.VMEM((planes - 1, K, K), F32),
            dma((chunks,)), dma((heads - 1,)), dma((heads,)),
            dma((n_up, PIECES)), dma((n_up, PIECES)), dma((n_dn, PIECES)), dma((n_dn, PIECES)),
            dma((heads - 1,)), dma((heads,)),
            dma((chunks, 6)), dma((chunks, 2)), dma((chunks, 4)),
            dma((heads - 1,)), dma((heads,)), dma((planes - 1,)), dma((1,)),
        ],
        compiler_params=pltpu.CompilerParams(
            collective_id=1, has_side_effects=True, vmem_limit_bytes=50 * 1024 * 1024
        ),
        name="whole",
    )(queries, keys, vals, small, out_weight)


def per_device(
    queries, key_vectors, values, beta_rates, log_gate, norm_gain, out_weight, decode_owner
):
    heads = log_gate.shape[1]
    planes = lax.axis_size("seq") // heads
    tokens = queries.shape[0]
    lines = 4 * heads

    def laid(x, first):
        return jnp.pad(x, ((first, lines - first - x.shape[0]), (0, tokens - x.shape[1])))

    small = (
        laid(log_gate.T, 0) + laid(beta_rates.T, heads) + laid(norm_gain.reshape(1, K), 3 * heads)
        + laid(decode_owner, 3 * heads + 1).astype(F32)
    )
    return whole(
        queries, key_vectors.transpose(1, 0, 2), values.transpose(1, 0, 2), small, out_weight,
        heads, planes, lax.axis_size("head"),
    )


def solution(mesh):
    in_specs = (
        P("seq", "head"), P("seq", None, "head"), P("seq", None, "head"), P("seq", "head"),
        P("seq", "head"), P(), P("head", None), P(None, "head"),
    )
    out_specs = (P(("seq", "head"), None), P("seq", "head", None, None))
    return jax.shard_map(
        per_device, mesh=mesh, in_specs=in_specs, out_specs=out_specs, check_vma=False
    )
```

```python
import functools
import jax
import jax.numpy as jnp
from jax import lax
from jax.experimental import pallas as pl
from jax.experimental.pallas import tpu as pltpu
from jax.sharding import PartitionSpec as P

K = 128
TB = 64
ROWS = 2 * TB
SUB = 8
F32 = jnp.float32
BF16 = jnp.bfloat16


def split(x):
    hi = x.astype(BF16)
    return hi, (x - hi.astype(F32)).astype(BF16)


def bdot(a, b):
    if a.ndim == 2:
        return lax.dot_general(a, b, (((1,), (0,)), ((), ())), preferred_element_type=F32)
    return lax.dot_general(a, b, (((2,), (1,)), ((0,), (0,))), preferred_element_type=F32)


def mm3(a, b):
    ah, al = a if isinstance(a, tuple) else split(a)
    bh, bl = b if isinstance(b, tuple) else split(b)
    wide = jnp.concatenate([ah, al, ah], axis=-1)
    tall = jnp.concatenate([bh, bh, bl], axis=-2)
    return bdot(wide, tall)


def twin(a, b):
    n, m, k = a.shape
    ah, al = split(a)
    bh, bl = b if isinstance(b, tuple) else split(b)
    wide = jnp.concatenate([ah, al, ah], axis=-1).reshape(n // 2, 2 * m, 3 * k)
    bh, bl = [jnp.concatenate([x.reshape(n // 2, 2, k, k)[:, t] for t in range(2)], axis=-1) for x in (bh, bl)]
    got = bdot(wide, jnp.concatenate([bh, bh, bl], axis=-2))
    return jnp.stack([got[:, :m, :k], got[:, m:, k:]], axis=1).reshape(n, m, k)


def iota(shape, dim):
    return lax.broadcasted_iota(jnp.int32, shape, dim)


MESH = pl.DeviceIdType.MESH
PIECES = 4
GROUP = 4


def place(wide_c):
    return jnp.concatenate([wide_c, jnp.zeros(wide_c.shape, F32)], axis=-1)


def masks():
    r_i, s_i = iota((ROWS, ROWS), 0), iota((ROWS, ROWS), 1)
    return r_i, s_i, r_i % TB, s_i % TB


def decays(run, run_lane):
    seen = iota((TB, ROWS), 1) % TB <= iota((TB, ROWS), 0)
    return jnp.where(seen, jnp.exp(jnp.where(seen, run - run_lane, 0.0)), 0.0)


def odd_rows(x, size, which=1):
    groups = x.reshape(x.shape[0], ROWS // (2 * size), 2, size, x.shape[-1])
    return groups[:, :, which].reshape(x.shape[0], ROWS // 2, x.shape[-1])


def among_odd(odd, even, size):
    shape = (odd.shape[0], ROWS // (2 * size), 1, size, odd.shape[-1])
    both = jnp.concatenate([even.reshape(shape), odd.reshape(shape)], axis=2)
    return both.reshape(odd.shape[0], ROWS, odd.shape[-1])


def three(x):
    one = x.astype(BF16).astype(F32)
    two = (x - one).astype(BF16).astype(F32)
    return [one, two, x - one - two]


def invert(system, nb, r_t, s_t):
    near = (r_t // SUB) == (s_t // SUB)
    folded = jnp.sum(
        jnp.where(near, system, 0.0).reshape(nb, 2, TB // SUB, SUB, ROWS), axis=2
    ).reshape(nb * 2 * SUB, ROWS)
    e_i, e_l = iota((2 * SUB, ROWS), 0), iota((2 * SUB, ROWS), 1)
    eye = jnp.where(((e_i // SUB) == (e_l // TB)) & ((e_i % SUB) == (e_l % SUB)), 1.0, 0.0).astype(F32)
    inv = jnp.broadcast_to(eye, (nb, 2 * SUB, ROWS))
    base = (iota((nb * 2 * SUB, ROWS), 1) % TB) // SUB * SUB
    for i in range(SUB):
        for j in range(2):
            if i == SUB - 1 and j == 1:
                continue
            factor = jnp.take_along_axis(folded, base + (j * TB + i), axis=1, mode="promise_in_bounds")
            factor = factor.reshape(nb, 2 * SUB, ROWS)
            at = j * SUB + i
            inv = inv - factor * inv[:, at:at + 1, :]
    solve = jnp.broadcast_to(
        inv.reshape(nb, 2, 1, SUB, ROWS), (nb, 2, TB // SUB, SUB, ROWS)
    ).reshape(nb, ROWS, ROWS)
    solve = jnp.where(near, solve, 0.0)
    size = SUB
    while size < TB:
        pair = ((r_t // (2 * size)) == (s_t // (2 * size))) & ((r_t // size) > (s_t // size))
        later = odd_rows(solve, size)
        crossed = twin(odd_rows(jnp.where(pair, system, 0.0), size), solve)
        later = later - twin(later, among_odd(crossed, jnp.zeros_like(crossed), size))
        solve = among_odd(later, odd_rows(solve, size, 0), size)
        size *= 2
    return solve


def whole_kernel(
    planes, q_buf, k_ref, v_ref, small_ref, w_ref,
    out_ref, states_ref, taken, w_buf, col_scr, row_scr, sp, total_buf, gath, rows_hi, rows_lo,
    kt_hi, kt_lo, carry, reach_hi, reach_lo, base_scr, from_low, from_high, out_buf, in_buf, end_buf,
    normed, part, relay, landed, finals, chosen,
    w_sem, send_a, recv_a, send_up, recv_up, send_dn, recv_dn, send_c, recv_c,
    send_sem, relay_sem, land_sem, share_send, share_recv, give_send, give_recv,
):
    tokens = small_ref.shape[1]
    heads = sp.shape[0]
    nb = tokens // TB
    chunks, depth, width = w_buf.shape
    half = width // 2
    ring = part.shape[2]
    rows = tokens // ring
    seq, me = lax.axis_index("seq"), lax.axis_index("head")
    z, i = seq // heads, lax.rem(seq, heads)
    at_end = z == planes - 1
    up = (lax.rem(z + 1, planes) * heads + i, me)
    down = (lax.rem(z + planes - 1, planes) * heads + i, me)
    n_up, n_dn = from_low.shape[0], from_high.shape[0]
    right, left = lax.rem(me + 1, ring), lax.rem(me + ring - 1, ring)
    far = lax.rem(me + 2, ring)

    def peer(offset):
        return lax.rem(i + offset, heads)

    def load(c):
        return pltpu.make_async_copy(w_ref.at[:, pl.ds(c * width, width)], w_buf.at[c], w_sem.at[c])

    pairs = heads // GROUP

    for c in range(chunks):
        load(c).start()

    barrier = pltpu.get_barrier_semaphore()
    for offset in range(1, heads):
        pl.semaphore_signal(barrier, inc=1, device_id=(z * heads + peer(offset), me), device_id_type=MESH)
    for where in (up, down, (seq, right), (seq, left)):
        pl.semaphore_signal(barrier, inc=1, device_id=where, device_id_type=MESH)

    @pl.when(z != planes - 1)
    def _():
        source = (planes - 1) * heads + i
        pl.semaphore_signal(barrier, inc=1, device_id=(source, me), device_id_type=MESH)

    gate = small_ref[0:heads]
    t_i, s_i = iota((tokens, tokens), 0), iota((tokens, tokens), 1)
    upto = jnp.where(((t_i // TB) == (s_i // TB)) & (s_i <= t_i), 1.0, 0.0).astype(F32)
    run = lax.dot_general(
        gate, upto, (((1,), (1,)), ((), ())), precision=lax.Precision.HIGHEST, preferred_element_type=F32
    )
    terms = jnp.concatenate(three(small_ref[heads:3 * heads]) + three(run), axis=0).astype(BF16)
    same = jnp.where(t_i == s_i, 1.0, 0.0).astype(BF16)
    col_scr[...] = lax.dot_general(
        same, terms, (((1,), (1,)), ((), ())), preferred_element_type=F32
    ).astype(BF16)
    row_scr[...] = jnp.concatenate(
        [run[:, b // 2 * TB:(b // 2 + 1) * TB] for b in range(2 * nb)], axis=1
    )

    batch = GROUP * nb

    def columns(h0, kinds):
        shape = (9 * heads, K)
        at = iota(shape, 0)
        rate_at, run_at = jnp.where(at < 6 * heads, at % (2 * heads), -1), jnp.where(at < 6 * heads, -1, at % heads)
        picks = []
        for kind in kinds:
            for g in range(GROUP):
                hit = (run_at == h0 + pairs * g) if kind == 2 else (rate_at == 2 * (h0 + pairs * g) + kind)
                picks.append(jnp.where(hit, 1.0, 0.0).astype(BF16))
        got = lax.dot_general(
            col_scr[...], jnp.concatenate(picks, axis=1), (((1,), (0,)), ((), ())), preferred_element_type=F32
        )
        tiles = [got[:, n * K:(n + 1) * K].reshape(nb, TB, K) for n in range(len(picks))]
        return [jnp.concatenate(tiles[n:n + GROUP], axis=0) for n in range(0, len(picks), GROUP)]

    def lane_rows(h0):
        got = []
        for g in range(GROUP):
            picked = jnp.sum(
                jnp.where(iota((heads, nb * ROWS), 0) == h0 + pairs * g, row_scr[...], 0.0), axis=0, keepdims=True
            )
            got += [picked[:, b * ROWS:(b + 1) * ROWS] for b in range(nb)]
        return jnp.stack(got, axis=0)

    def head_cols(h):
        return pl.ds(pl.multiple_of(h * K, K), K)

    def by_head(ref, h0):
        return jnp.concatenate(
            [ref[:, head_cols(h0 + pairs * g)].astype(F32).reshape(nb, TB, K) for g in range(GROUP)], axis=0
        )

    def unit(x):
        return x * lax.rsqrt(jnp.sum(x * x, axis=-1, keepdims=True) + 1e-6)

    def give_a(h):
        where = jnp.where(h > i, h - 1, h)
        return pltpu.make_async_remote_copy(
            src_ref=sp.at[h], dst_ref=gath.at[i], send_sem=send_a.at[where],
            recv_sem=recv_a.at[i], device_id=(z * heads + h, me), device_id_type=MESH,
        )

    def transition(step, _):
        pair = h0 = step
        rate0, rate1, run = columns(h0, (0, 1, 2))
        run_lane = lane_rows(h0)
        closing = run_lane[:, :, ROWS - 1:ROWS]
        rates = jnp.concatenate([rate0, rate1], axis=1)
        key = unit(jnp.concatenate([by_head(k_ref.at[j], h0) for j in range(2)], axis=1))
        val = jnp.concatenate([by_head(v_ref.at[j], h0) for j in range(2)], axis=1)
        key_t = jnp.stack([key[b].T for b in range(batch)], axis=0)
        kth, ktl = split(key_t)
        kt_hi[pair], kt_lo[pair] = kth, ktl
        decay = decays(run, run_lane)
        r_i, s_i, r_t, s_t = masks()
        below = (r_t > s_t) | ((r_t == s_t) & (r_i > s_i))
        gram = twin(key, (kth, ktl))
        system = jnp.where(below, rates * jnp.concatenate([decay, decay], axis=1) * gram, 0.0)
        solve = invert(system, batch, r_t, s_t)
        grown = jnp.exp(jnp.concatenate([run, run], axis=1))
        got = split(mm3(solve, jnp.concatenate([rates * val, (rates * grown) * key], axis=2)))
        rows_hi[pair], rows_lo[pair] = got
        z_rows = mm3(key_t * jnp.exp(closing - run_lane), got)
        k_i, k_j = iota((K, K), 0), iota((K, K), 1)
        ident = jnp.where(k_i == k_j, 1.0, 0.0).astype(F32)
        move = (jnp.exp(closing) * ident - z_rows[:, :, K:]).reshape(GROUP, nb, K, K)
        fresh = z_rows[:, :, :K].reshape(GROUP, nb, K, K)
        state = jnp.concatenate([fresh[:, 0], move[:, 0]], axis=2)
        for b in range(1, nb):
            carry[pair, b - 1] = state
            state = mm3(move[:, b], state) + place(fresh[:, b])
        for g in range(GROUP):
            sp[h0 + pairs * g] = state[g]

        @pl.when((step == 0) & at_end)
        def _():
            pl.semaphore_wait(barrier, heads + 3 + planes - 1)

        @pl.when((step == 0) & (z != planes - 1))
        def _():
            pl.semaphore_wait(barrier, heads + 3)

        for g in range(GROUP):
            @pl.when(h0 + pairs * g != i)
            def _():
                give_a(h0 + pairs * g).start()

            @pl.when(h0 + pairs * g == i)
            def _():
                gath[i] = state[g]

        return 0

    lax.fori_loop(0, pairs, transition, 0)

    def reaches(pair, _):
        h0 = pair
        (run,) = columns(h0, (2,))
        query = by_head(q_buf, h0)
        scores = twin(query, (kt_hi[pair], kt_lo[pair])) * decays(run, lane_rows(h0))
        z_out = mm3(scores, (rows_hi[pair], rows_lo[pair])).reshape(GROUP, nb, TB, 2 * K)
        reach = (jnp.exp(run) * query).reshape(GROUP, nb, TB, K) - z_out[..., K:]
        base = [z_out[:, 0, :, :K]]
        whole_reach = [reach[:, 0]]
        for b in range(1, nb):
            both = mm3(reach[:, b], carry[pair, b - 1])
            base.append(both[:, :, :K] + z_out[:, b, :, :K])
            whole_reach.append(both[:, :, K:])
        base_scr[pair] = jnp.concatenate(base, axis=1)
        reach_hi[pair], reach_lo[pair] = split(jnp.concatenate(whole_reach, axis=1))
        return 0

    early = jnp.where(lax.rem(i, pairs) == 0, 0, pairs)
    lax.fori_loop(0, early, reaches, 0)
    for src in range(heads):
        @pl.when(src != i)
        def _():
            pltpu.make_async_copy(gath.at[src], gath.at[src], recv_a.at[src]).wait()
    def compose(later, earlier):
        return mm3(later[..., K:], earlier) + place(later[..., :K])

    odd = gath[1], gath[3], gath[5], gath[7]
    twos = compose(jnp.stack(odd), jnp.stack([gath[0], gath[2], gath[4], gath[6]]))
    fours = compose(jnp.stack([twos[1], twos[3]]), jnp.stack([twos[0], twos[2]]))
    total_buf[...] = compose(fours[1], fours[0])

    bit = K // PIECES

    def hop(s, p, upward):
        slots = from_low if upward else from_high
        src = total_buf if s == 0 else slots.at[s - 1]
        send, recv = (send_up, recv_up) if upward else (send_dn, recv_dn)
        lines = pl.ds(p * bit, bit)
        return pltpu.make_async_remote_copy(
            src_ref=src.at[lines], dst_ref=slots.at[s, lines], send_sem=send.at[s, p],
            recv_sem=recv.at[s, p], device_id=up if upward else down, device_id_type=MESH,
        )

    for p in range(PIECES):
        hop(0, p, True).start()
        hop(0, p, False).start()
    firsts = compose(jnp.stack([gath[2], gath[4], twos[2]]), jnp.stack([twos[0], fours[0], fours[0]]))
    gath[6] = compose(gath[6], firsts[2])
    gath[1], gath[3] = twos[0], fours[0]
    gath[2], gath[4], gath[5] = firsts[0], firsts[1], firsts[2]
    gath[7] = total_buf[...]
    k_i, k_j = iota((K, 2 * K), 0), iota((K, 2 * K), 1)
    acc = jnp.where(k_i + K == k_j, 1.0, 0.0).astype(F32)
    state = jnp.zeros((K, K), F32)
    for s in range(n_up):
        if s == 0:
            lax.fori_loop(early, pairs, reaches, 0)
        if s == n_up - 1:
            prefix = gath[...]
            near = mm3(prefix[:, :, K:].reshape(heads * K, K), acc).reshape(heads, K, 2 * K)
            ready = jnp.concatenate([acc[None], near + place(prefix[:, :, :K])], axis=0)
        for p in range(PIECES):
            hop(s, p, True).wait_recv()
            if s + 1 < n_up:
                hop(s + 1, p, True).start()
            if s < n_dn:
                hop(s, p, False).wait_recv()
                if s + 1 < n_dn:
                    hop(s + 1, p, False).start()
        earlier = from_low[s]
        if s == n_up - 1:
            moved = mm3(earlier[:, K:], state) + earlier[:, :K]
            state = jnp.where(z >= n_up, moved, state)
            break
        joined = earlier if s == 0 else mm3(acc[:, K:], earlier) + place(acc[:, :K])
        acc = jnp.where(z >= s + 1, joined, acc)
        if s < n_dn:
            wrapped = from_high[s]
            moved = wrapped[:, :K] if s == 0 else mm3(wrapped[:, K:], state) + wrapped[:, :K]
            state = jnp.where(z + s + 1 >= planes, moved, state)
    spread_out = mm3(ready[:, :, K:].reshape((heads + 1) * K, K), state).reshape(heads + 1, K, K)
    spread_out = spread_out + ready[:, :, :K]
    out_buf[...] = spread_out[:heads]
    end_buf[...] = spread_out[heads]

    def give_c(offset):
        other = peer(offset)
        return pltpu.make_async_remote_copy(
            src_ref=out_buf.at[other], dst_ref=in_buf.at[lax.rem(i, pairs), i // pairs], send_sem=send_c.at[offset - 1],
            recv_sem=recv_c.at[i], device_id=(z * heads + other, me), device_id_type=MESH,
        )

    def share(offset):
        other = peer(offset)
        return pltpu.make_async_remote_copy(
            src_ref=end_buf, dst_ref=finals.at[i], send_sem=share_send.at[offset - 1],
            recv_sem=share_recv.at[i], device_id=(z * heads + other, me), device_id_type=MESH,
        )

    def give(plane):
        return pltpu.make_async_remote_copy(
            src_ref=chosen.at[plane], dst_ref=taken, send_sem=give_send.at[plane],
            recv_sem=give_recv.at[0], device_id=(plane * heads + i, me), device_id_type=MESH,
        )

    for offset in range(1, heads):
        give_c(offset).start()
    in_buf[lax.rem(i, pairs), i // pairs] = out_buf[i]

    @pl.when(at_end)
    def _():
        finals[i] = end_buf[...]
        for offset in range(1, heads):
            share(offset).start()

    gain = small_ref[3 * heads:3 * heads + 1, 0:K]

    def owned(device):
        owners = small_ref[3 * heads + 1:3 * heads + 3, 0:heads]
        found = jnp.where(owners == lax.convert_element_type(device, F32), 1.0, 0.0).astype(F32)
        return jnp.max(found, axis=0, keepdims=True)


    def attend(step, _):
        for g in range(GROUP):
            h = step + pairs * g

            @pl.when(h != i)
            def _():
                here = in_buf.at[step, g]
                pltpu.make_async_copy(here, here, recv_c.at[h]).wait()

        attended = base_scr[step] + mm3((reach_hi[step], reach_lo[step]), in_buf[step])
        scale = lax.rsqrt(jnp.mean(attended * attended, axis=-1, keepdims=True) + 1e-6)
        got = (attended * scale * gain).astype(BF16)
        for g in range(GROUP):
            normed[:, head_cols(step + pairs * g)] = got[g]
        return 0

    lax.fori_loop(0, pairs, attend, 0)

    def push(src, dst, kind, c, recv, where):
        return pltpu.make_async_remote_copy(
            src_ref=src, dst_ref=dst, send_sem=send_sem.at[c, kind], recv_sem=recv,
            device_id=(seq, where), device_id_type=MESH,
        )

    def far_a(c):
        return push(part.at[c, 0, far], relay.at[c, 0], 0, c, relay_sem.at[c, 0], right)

    def far_b(c):
        return push(part.at[c, 1, far], relay.at[c, 1], 1, c, relay_sem.at[c, 1], left)

    def near_b(c):
        return push(part.at[c, 1, right], landed.at[c, 1], 2, c, land_sem.at[c, 1], right)

    def near_a(c):
        return push(part.at[c, 0, left], landed.at[c, 2], 3, c, land_sem.at[c, 2], left)

    def sum_a(c):
        return push(part.at[c, 0, right], landed.at[c, 0], 4, c, land_sem.at[c, 0], right)

    def sum_b(c):
        return push(part.at[c, 1, left], landed.at[c, 3], 5, c, land_sem.at[c, 3], left)

    def merge(c):
        far_a(c).wait_recv()
        part[c, 0, right] = part[c, 0, right] + relay[c, 0]
        sum_a(c).start()
        far_b(c).wait_recv()
        part[c, 1, left] = part[c, 1, left] + relay[c, 1]
        sum_b(c).start()
        return 0

    def compute(c):
        load(c).wait()
        got = lax.dot_general(
            normed[...], w_buf[c], (((1,), (0,)), ((), ())), preferred_element_type=F32
        )
        part[c, 0] = got[:, :half].reshape(ring, rows, half)
        part[c, 1] = got[:, half:].reshape(ring, rows, half)
        far_a(c).start()
        far_b(c).start()
        return 0

    lax.fori_loop(0, chunks, lambda c, _: compute(c), 0)

    def near(c, _):
        near_b(c).start()
        near_a(c).start()
        return 0

    lax.fori_loop(0, chunks, near, 0)
    lax.fori_loop(0, chunks, lambda c, _: merge(c), 0)

    @pl.when(at_end)
    def _():
        for offset in range(1, heads):
            other = lax.rem(i + offset, heads)
            pltpu.make_async_copy(finals.at[other], finals.at[other], share_recv.at[other]).wait()
        for plane in range(planes):
            picked = owned(plane * heads + i)
            total = finals[0] * picked[:, 0:1]
            for h in range(1, heads):
                total = total + finals[h] * picked[:, h:h + 1]
            if plane < planes - 1:
                chosen[plane] = total
                give(plane).start()
            else:
                taken[...] = total

    def finish(c, _):
        for copy in (sum_a(c), near_b(c), near_a(c), sum_b(c)):
            copy.wait_recv()
        one = part[c, 0, me] + landed[c, 0] + landed[c, 2]
        two = part[c, 1, me] + landed[c, 1] + landed[c, 3]
        out_ref[:, pl.ds(pl.multiple_of(c * width, width), width)] = jnp.concatenate(
            [one, two], axis=1
        ).astype(out_ref.dtype)
        for copy in (far_a(c), far_b(c), near_b(c), near_a(c), sum_a(c), sum_b(c)):
            copy.wait_send()
        return 0

    lax.fori_loop(0, chunks, finish, 0)

    @pl.when(at_end)
    def _():
        for offset in range(1, heads):
            share(offset).wait_send()
        for plane in range(planes - 1):
            give(plane).wait_send()

    @pl.when(z != planes - 1)
    def _():
        give(0).wait_recv()

    mine = owned(seq)
    for h in range(heads):
        states_ref[0, h] = taken[...] * mine[:, h:h + 1]

    for offset in range(1, heads):
        give_a(peer(offset)).wait_send()
        give_c(offset).wait_send()
    for p in range(PIECES):
        for s in range(n_up):
            hop(s, p, True).wait_send()
        for s in range(n_dn):
            hop(s, p, False).wait_send()


def whole(queries, keys, vals, small, out_weight, heads, planes, ring, chunks=4):
    tokens, wide = queries.shape
    nb = tokens // TB
    depth, columns = out_weight.shape
    width = columns // chunks
    rows, half = tokens // ring, width // 2
    n_up, n_dn = planes // 2, planes - 1 - planes // 2
    dma = pltpu.SemaphoreType.DMA
    vmem = pl.BlockSpec(memory_space=pltpu.VMEM)
    hbm = pl.BlockSpec(memory_space=pltpu.HBM)
    pair = (heads, K, 2 * K)
    return pl.pallas_call(
        functools.partial(whole_kernel, planes),
        in_specs=[vmem, vmem, vmem, vmem, hbm],
        out_specs=[vmem, vmem],
        out_shape=[
            jax.ShapeDtypeStruct((rows, columns), BF16),
            jax.ShapeDtypeStruct((1, heads, K, K), F32),
        ],
        scratch_shapes=[
            pltpu.VMEM((K, K), F32),
            pltpu.VMEM((chunks, depth, width), BF16),
            pltpu.VMEM((tokens, 9 * heads), BF16),
            pltpu.VMEM((heads, nb * ROWS), F32),
            pltpu.VMEM(pair, F32),
            pltpu.VMEM((K, 2 * K), F32),
            pltpu.VMEM(pair, F32),
            pltpu.VMEM((heads // GROUP, GROUP * nb, ROWS, 2 * K), BF16),
            pltpu.VMEM((heads // GROUP, GROUP * nb, ROWS, 2 * K), BF16),
            pltpu.VMEM((heads // GROUP, GROUP * nb, K, ROWS), BF16),
            pltpu.VMEM((heads // GROUP, GROUP * nb, K, ROWS), BF16),
            pltpu.VMEM((heads // GROUP, nb - 1, GROUP, K, 2 * K), F32),
            pltpu.VMEM((heads // GROUP, GROUP, tokens, K), BF16),
            pltpu.VMEM((heads // GROUP, GROUP, tokens, K), BF16),
            pltpu.VMEM((heads // GROUP, GROUP, tokens, K), F32),
            pltpu.VMEM((n_up, K, 2 * K), F32),
            pltpu.VMEM((n_dn, K, 2 * K), F32),
            pltpu.VMEM((heads, K, K), F32),
            pltpu.VMEM((heads // GROUP, GROUP, K, K), F32),
            pltpu.VMEM((K, K), F32),
            pltpu.VMEM((tokens, depth), BF16),
            pltpu.VMEM((chunks, 2, ring, rows, half), F32),
            pltpu.VMEM((chunks, 2, rows, half), F32),
            pltpu.VMEM((chunks, 4, rows, half), F32),
            pltpu.VMEM((heads, K, K), F32),
            pltpu.VMEM((planes - 1, K, K), F32),
            dma((chunks,)), dma((heads - 1,)), dma((heads,)),
            dma((n_up, PIECES)), dma((n_up, PIECES)), dma((n_dn, PIECES)), dma((n_dn, PIECES)),
            dma((heads - 1,)), dma((heads,)),
            dma((chunks, 6)), dma((chunks, 2)), dma((chunks, 4)),
            dma((heads - 1,)), dma((heads,)), dma((planes - 1,)), dma((1,)),
        ],
        compiler_params=pltpu.CompilerParams(
            collective_id=1, has_side_effects=True, vmem_limit_bytes=50 * 1024 * 1024
        ),
        name="whole",
    )(queries, keys, vals, small, out_weight)


def per_device(
    queries, key_vectors, values, beta_rates, log_gate, norm_gain, out_weight, decode_owner
):
    heads = log_gate.shape[1]
    planes = lax.axis_size("seq") // heads
    tokens = queries.shape[0]
    lines = 4 * heads

    def laid(x, first):
        return jnp.pad(x, ((first, lines - first - x.shape[0]), (0, tokens - x.shape[1])))

    small = (
        laid(log_gate.T, 0) + laid(beta_rates.T, heads) + laid(norm_gain.reshape(1, K), 3 * heads)
        + laid(decode_owner, 3 * heads + 1).astype(F32)
    )
    return whole(
        queries, key_vectors.transpose(1, 0, 2), values.transpose(1, 0, 2), small, out_weight,
        heads, planes, lax.axis_size("head"),
    )


def solution(mesh):
    in_specs = (
        P("seq", "head"), P("seq", None, "head"), P("seq", None, "head"), P("seq", "head"),
        P("seq", "head"), P(), P("head", None), P(None, "head"),
    )
    out_specs = (P(("seq", "head"), None), P("seq", "head", None, None))
    return jax.shard_map(
        per_device, mesh=mesh, in_specs=in_specs, out_specs=out_specs, check_vma=False
    )
```
